256 devices in a mesh: dp: 8 (over y, core), seq: 32 (over z, x).
Axes of the slice: x: 4, y: 4, z: 8, core: 2. Of those that a mesh axis runs over, the one named last changes fastest.
Arguments:
- queries: bfloat16 [8, 4096, 1152], P('dp', 'seq'), may hold values from -12 to 12
- keys: bfloat16 [8, 4096, 1152], P('dp', 'seq'), may hold values from -12 to 12
- values: bfloat16 [8, 4096, 1152], P('dp', 'seq'), may hold values from -6 to 6
- out_weight: bfloat16 [1152, 1152], replicated, may hold values from -0.1875 to 0.1875
- out_grad: bfloat16 [8, 4096, 1152], P('dp', 'seq'), may hold values from -48 to 48
- lengths: int32 [8, 20], P('dp'), may hold values from 128 to 384, as said below
Outputs:
- query_grad: float32 [8, 4096, 1152], P('dp', 'seq')
- key_grad: float32 [8, 4096, 1152], P('dp', 'seq')
- value_grad: float32 [8, 4096, 1152], P('dp', 'seq')
- weight_grad: float32 [1152, 1152], P('seq')
The draws below stay inside these ranges and needn't reach their ends.
Inputs may be any that keep to these rules, and one draw needn't show every extreme that they name: Each row's 20 lengths sum to 4096; the largest in each row is exactly 384.
All inputs are finite; a program needn't handle non-finite values.
Results may differ from the reference program's by a relative error of at most 0.012.
The reference program's roundings to bfloat16 on the way count: a program that leaves them out, or rounds other values in their place, can miss the bound.
Values may be sent and summed in bfloat16 or wider, within the bound.
A program may use at most 128 MiB of HBM per device.

```python
import jax
import jax.numpy as jnp
from jax import lax

D = 1152
HEADS = 16
HEAD_DIM = 72
TOK_DEV = 128
MAXLEN = 384
BATCH = 8
TOKENS = 4096
NIMG = 20
REACH = 3
ALL_TOK = 32768


def draw_queries(key, part):
    drawn = jnp.clip(jax.random.normal(jax.random.fold_in(key, 1), (BATCH, TOKENS, D), jnp.float32), -6.0, 6.0)
    return jnp.clip(drawn, -12.0, 12.0).astype(jnp.bfloat16)


def draw_keys(key, part):
    drawn = jnp.clip(jax.random.normal(jax.random.fold_in(key, 2), (BATCH, TOKENS, D), jnp.float32), -6.0, 6.0)
    return jnp.clip(drawn, -12.0, 12.0).astype(jnp.bfloat16)


def draw_lengths(key, part):
    least = MAXLEN // 3
    ceiling = MAXLEN - least
    count = NIMG - 1
    extra = TOKENS - MAXLEN - count * least
    share = extra // count
    remain = extra - share * count
    spread = max(min(share, ceiling - share), 1)
    pairs = count // 2

    def one_row(row):
        row_key = jax.random.fold_in(key, row)
        order_perm = jax.random.permutation(jax.random.fold_in(row_key, 1), count).astype(jnp.int32)
        amount = jax.random.randint(jax.random.fold_in(row_key, 2), (pairs,), 0, spread, dtype=jnp.int32)
        amount = amount.at[0].set(share)
        delta = jnp.zeros((count,), jnp.int32)
        delta = delta.at[order_perm[0:2 * pairs:2]].add(amount)
        delta = delta.at[order_perm[1:2 * pairs:2]].add(-amount)
        bump_order = jnp.concatenate([order_perm[0:1], order_perm[2:], order_perm[1:2]])
        bumps = (jnp.arange(count, dtype=jnp.int32) < remain).astype(jnp.int32)
        delta = delta.at[bump_order].add(bumps)
        others = least + share + delta
        place = jax.random.randint(jax.random.fold_in(row_key, 3), (), 0, NIMG, dtype=jnp.int32)
        slots = jnp.arange(NIMG, dtype=jnp.int32)
        source = jnp.clip(jnp.where(slots < place, slots, slots - 1), 0, count - 1)
        return jnp.where(slots == place, MAXLEN, others[source]).astype(jnp.int32)
    return lax.map(one_row, jnp.arange(BATCH, dtype=jnp.int32))


def levels(stream_key, dims, pieces, low, largest):
    def one(position, shards_of):
        draws = jax.random.uniform(jax.random.fold_in(jax.random.fold_in(stream_key, 6), position), (shards_of,), jnp.float32, low / len(pieces), largest / len(pieces))
        return jnp.repeat(jnp.exp(draws), dims[position] // shards_of).reshape((-1,) + (1,) * (len(dims) - position - 1))

    gain = one(*pieces[0])
    for cut in pieces[1:]:
        gain = gain * one(*cut)
    return gain


def bell_draw(key, dims, width, limit, split=(), kind=jnp.bfloat16):
    values = jax.random.normal(key, dims, jnp.float32) * width
    if len(split) > 0:
        values = levels(key, dims, split, -0.22, 0.18) * values
    return jnp.clip(values, min=-limit, max=limit).astype(kind)


def setup_inputs(seed: int = 0) -> dict:
    key_list = jax.random.split(jax.random.key(seed), 7)
    queries = draw_queries(jax.random.fold_in(key_list[6], 71), 0)
    keys = draw_keys(jax.random.fold_in(key_list[6], 71), 0)
    values = bell_draw(key_list[2], (BATCH, TOKENS, D), 1.0, 6.0, ((0, 8), (1, 32)))
    out_weight = bell_draw(key_list[3], (D, D), D ** -0.5, 0.1875)
    out_grad = bell_draw(key_list[4], (BATCH, TOKENS, D), 8.0, 48.0, ((0, 8), (1, 32)))
    lengths = draw_lengths(jax.random.fold_in(key_list[6], 71), 0)
    return dict(queries=queries, keys=keys, values=values, out_weight=out_weight, out_grad=out_grad, lengths=lengths)


def reference(queries, keys, values, out_weight, out_grad, lengths):
    score_scale = HEAD_DIM ** -0.5
    pad_rows = REACH * TOK_DEV
    window = (2 * REACH + 1) * TOK_DEV

    def one_group(inputs):
        q_all, k_all, v_all, dy_all, lens_row = inputs
        image_ends = jnp.cumsum(lens_row).astype(jnp.int32)
        positions = jnp.arange(TOKENS, dtype=jnp.int32)
        image_ids = jnp.sum((positions[:, None] >= image_ends[None, :]).astype(jnp.int32), axis=1).astype(jnp.int32)
        keys_pad = jnp.pad(k_all, ((pad_rows, pad_rows), (0, 0)))
        values_pad = jnp.pad(v_all, ((pad_rows, pad_rows), (0, 0)))
        ids_pad = jnp.pad(image_ids, (pad_rows, pad_rows), constant_values=-1).astype(jnp.int32)
        d_all = jnp.dot(dy_all, out_weight.T, preferred_element_type=jnp.float32).astype(jnp.bfloat16)

        def block_step(carried, block):
            k_grads, v_grads, w_grad = carried
            start = (block * TOK_DEV).astype(jnp.int32)
            q_blk = lax.dynamic_slice_in_dim(q_all, start, TOK_DEV, 0)
            d_blk = lax.dynamic_slice_in_dim(d_all, start, TOK_DEV, 0)
            dy_blk = lax.dynamic_slice_in_dim(dy_all, start, TOK_DEV, 0)
            q_ids = lax.dynamic_slice_in_dim(image_ids, start, TOK_DEV, 0)
            k_win = lax.dynamic_slice_in_dim(keys_pad, start, window, 0)
            v_win = lax.dynamic_slice_in_dim(values_pad, start, window, 0)
            k_ids = lax.dynamic_slice_in_dim(ids_pad, start, window, 0)
            q_heads = q_blk.astype(jnp.float32).reshape(TOK_DEV, HEADS, HEAD_DIM)
            k_heads = k_win.astype(jnp.float32).reshape(window, HEADS, HEAD_DIM)
            v_heads = v_win.astype(jnp.float32).reshape(window, HEADS, HEAD_DIM)
            d_heads = d_blk.astype(jnp.float32).reshape(TOK_DEV, HEADS, HEAD_DIM)
            scores = jnp.einsum('qhd,khd->hqk', q_heads, k_heads) * score_scale
            same_image = q_ids[:, None] == k_ids[None, :]
            scores = jnp.where(same_image[None, :, :], scores, -1.0e30)
            row_max = jnp.max(scores, axis=2)
            log_norm = row_max + jnp.log(jnp.sum(jnp.exp(scores - row_max[:, :, None]), axis=2))
            weights = jnp.exp(scores - log_norm[:, :, None]).astype(jnp.bfloat16)
            weights_f = weights.astype(jnp.float32)
            attended = jnp.einsum('hqk,khd->qhd', weights_f, v_heads).reshape(TOK_DEV, D).astype(jnp.bfloat16)
            row_delta = jnp.sum(d_heads * attended.astype(jnp.float32).reshape(TOK_DEV, HEADS, HEAD_DIM), axis=2).T
            d_probs = jnp.einsum('qhd,khd->hqk', d_heads, v_heads)
            d_scores = (score_scale * weights_f * (d_probs - row_delta[:, :, None])).astype(jnp.bfloat16)
            d_scores_f = d_scores.astype(jnp.float32)
            q_grad = jnp.einsum('hqk,khd->qhd', d_scores_f, k_heads).reshape(TOK_DEV, D)
            k_part = jnp.einsum('hqk,qhd->khd', d_scores_f, q_heads).reshape(window, D)
            v_part = jnp.einsum('hqk,qhd->khd', weights_f, d_heads).reshape(window, D)
            k_grads = lax.dynamic_update_slice_in_dim(k_grads, lax.dynamic_slice_in_dim(k_grads, start, window, 0) + k_part, start, 0)
            v_grads = lax.dynamic_update_slice_in_dim(v_grads, lax.dynamic_slice_in_dim(v_grads, start, window, 0) + v_part, start, 0)
            w_grad = w_grad + jnp.dot(attended.T, dy_blk, preferred_element_type=jnp.float32)
            return (k_grads, v_grads, w_grad), q_grad

        init = (jnp.zeros((TOKENS + 2 * pad_rows, D), jnp.float32), jnp.zeros((TOKENS + 2 * pad_rows, D), jnp.float32), jnp.zeros((D, D), jnp.float32))
        finals, q_blocks = lax.scan(block_step, init, jnp.arange(TOKENS // TOK_DEV, dtype=jnp.int32))
        k_grads, v_grads, w_grad = finals
        return q_blocks.reshape(TOKENS, D), k_grads[pad_rows:pad_rows + TOKENS], v_grads[pad_rows:pad_rows + TOKENS], w_grad

    query_grad, key_grad, value_grad, w_grads = lax.map(one_group, (queries, keys, values, out_grad, lengths))
    weight_grad = jnp.sum(w_grads, axis=0) * (ALL_TOK ** -0.5)
    return query_grad, key_grad, value_grad, weight_grad
```

```python
import functools

import jax
import jax.numpy as jnp
from jax import lax
from jax.experimental import pallas as pl
from jax.experimental.pallas import tpu as pltpu
from jax.sharding import PartitionSpec as P

NX, NZ = 4, 8
NY, NCORE = 4, 2
NDP = NY * NCORE
BLK = 128
HEADS, HD = 16, 72
HPD = HEADS // NX
FEAT = HPD * HD
D = HEADS * HD
REACH = 3
SLOTS = NX + 2 * REACH
NIMG = 20
TOKENS = 4096
ALL_TOK = 32768
SCALE = HD ** -0.5
NEG = -1e30
PADW = 80
CHUNK = 640
CSTEP = 512
NRED = 5
ROWS = D // (NX * NZ)

F32, BF16 = jnp.float32, jnp.bfloat16
MESH = pl.DeviceIdType.MESH
VM = pl.BlockSpec(memory_space=pltpu.VMEM)


def place():
    dp, seq = lax.axis_index("dp"), lax.axis_index("seq")
    return dp, lax.div(seq, NX), lax.rem(seq, NX)


def remote(src, dst, send, recv, device):
    return pltpu.make_async_remote_copy(
        src_ref=src, dst_ref=dst, send_sem=send, recv_sem=recv, device_id=device, device_id_type=MESH
    )


def hello(barrier, device):
    pl.semaphore_signal(barrier, inc=1, device_id=device, device_id_type=MESH)


def dot_nn(a, b):
    return lax.dot_general(a, b, (((1,), (0,)), ((), ())), preferred_element_type=F32)


def dot_nt(a, b):
    return lax.dot_general(a, b, (((1,), (1,)), ((), ())), preferred_element_type=F32)


def gather_kernel(
    q_ref, k_ref, v_ref, dy_ref, w_ref,
    qt_out, kt_out, vt_out, kr_out, vr_out, dt_out, dy_out,
    ksend, vsend, qsend, kwin, vwin, qwin, wbuf,
    x_send, x_recv, z_send, z_recv, w_sem,
):
    dp, z, x = place()
    up, down = lax.rem(z + 1, NZ), lax.rem(z + NZ - 1, NZ)
    barrier = pltpu.get_barrier_semaphore()
    order = (1, 3, 2)

    def xdev(o):
        return (dp, NX * z + lax.rem(x + o, NX))

    for o in order:
        hello(barrier, xdev(o))
    for zz in (up, down):
        hello(barrier, (dp, NX * zz + x))
    w_copy = pltpu.make_async_copy(w_ref.at[pl.ds(pl.multiple_of(FEAT * x, 32), FEAT)], wbuf, w_sem)
    w_copy.start()

    def turn(src, dst):
        for i in range(D // BLK):
            tile = src[0, :, i * BLK : (i + 1) * BLK].astype(F32)
            dst[i * BLK : (i + 1) * BLK, :] = tile.T.astype(BF16)

    def part(ref, xp):
        return ref.at[pl.ds(pl.multiple_of(FEAT * xp, 32), FEAT)]

    def x_copy(t, o, src, win, base):
        xp = lax.rem(x + o, NX)
        return remote(
            part(src, xp), win.at[base + x], x_send.at[t, o], x_recv.at[t, NX - o], xdev(o)
        )

    def x_wait(t, o, src, win, base):
        xp = lax.rem(x + o, NX)
        remote(part(src, xp), win.at[base + xp], x_send.at[t, o], x_recv.at[t, o], xdev(o)).wait_recv()

    def dy_copy(o):
        return remote(dy_ref.at[0], dy_out.at[x], x_send.at[3, o], x_recv.at[3, NX - o], xdev(o))

    turn(k_ref, ksend)
    pl.semaphore_wait(barrier, 5)
    for o in order:
        x_copy(0, o, ksend, kwin, REACH).start()
    turn(v_ref, vsend)
    for o in order:
        x_copy(1, o, vsend, vwin, REACH).start()
    turn(q_ref, qsend)
    for o in order:
        x_copy(2, o, qsend, qwin, 0).start()
    for o in order:
        dy_copy(o).start()
    mine = pl.ds(pl.multiple_of(FEAT * x, 32), FEAT)
    kwin[REACH + x] = ksend[mine, :]
    vwin[REACH + x] = vsend[mine, :]
    qwin[x] = qsend[mine, :]
    dy_out[x] = dy_ref[0]

    def z_up(t, xp, win):
        slot = xp + NX + REACH
        return remote(
            win.at[REACH + xp], win.at[slot], z_send.at[t, 0, xp], z_recv.at[t, 1, xp], (dp, NX * down + x)
        )

    def z_down(t, xp, win):
        slot = xp - 1
        return remote(
            win.at[REACH + xp], win.at[slot], z_send.at[t, 1, xp], z_recv.at[t, 0, xp], (dp, NX * up + x)
        )

    for t, src, win in ((0, ksend, kwin), (1, vsend, vwin)):
        for o in (0, 1, 3, 2):
            xp = lax.rem(x + o, NX)
            if o:
                x_wait(t, o, src, win, REACH)

            @pl.when(xp <= REACH - 1)
            def _():
                z_up(t, xp, win).start()

            @pl.when(xp >= 1)
            def _():
                z_down(t, xp, win).start()

    def unpack(win, slot, t_out, r_out):
        val = win[slot].astype(F32)
        for h in range(HPD):
            piece = val[h * HD : (h + 1) * HD]
            t_out[h, slot] = piece.astype(BF16)
            if r_out is not None:
                r_out[h, slot] = piece.T.astype(BF16)

    def unpack_kv(slot, carry):
        unpack(kwin, slot, kt_out, kr_out)
        unpack(vwin, slot, vt_out, vr_out)
        return carry

    lax.fori_loop(REACH, REACH + NX, unpack_kv, 0)
    for o in order:
        x_wait(2, o, qsend, qwin, 0)

    def unpack_q(slot, carry):
        unpack(qwin, slot, qt_out, None)
        return carry

    lax.fori_loop(0, NX, unpack_q, 0)

    for t, win in ((0, kwin), (1, vwin)):
        for xp in range(REACH):
            remote(
                win.at[REACH + xp], win.at[xp + NX + REACH], z_send.at[t, 0, xp], z_recv.at[t, 1, xp],
                (dp, NX * down + x),
            ).wait_recv()
            remote(
                win.at[REACH + xp + 1], win.at[xp], z_send.at[t, 1, xp + 1], z_recv.at[t, 0, xp + 1],
                (dp, NX * up + x),
            ).wait_recv()
    lax.fori_loop(0, REACH, unpack_kv, 0)
    lax.fori_loop(REACH + NX, SLOTS, unpack_kv, 0)

    w_copy.wait()
    for o in (0, 1, 3, 2):
        xp = lax.rem(x + o, NX)
        if o:
            remote(dy_ref.at[0], dy_out.at[xp], x_send.at[3, o], x_recv.at[3, o], xdev(o)).wait_recv()
        d_blk = dot_nt(wbuf[...], dy_out[xp])
        for h in range(HPD):
            dt_out[h, xp] = d_blk[h * HD : (h + 1) * HD].astype(BF16)

    for o in order:
        x_copy(0, o, ksend, kwin, REACH).wait_send()
        x_copy(1, o, vsend, vwin, REACH).wait_send()
        x_copy(2, o, qsend, qwin, 0).wait_send()
        dy_copy(o).wait_send()
    for t, win in ((0, kwin), (1, vwin)):
        for xp in range(REACH):
            z_up(t, xp, win).wait_send()
            z_down(t, xp + 1, win).wait_send()


def gather(queries, keys, values, out_grad, out_weight):
    heads_t = lambda n: jax.ShapeDtypeStruct((HPD, n, HD, BLK), BF16)
    heads_r = lambda n: jax.ShapeDtypeStruct((HPD, n, BLK, HD), BF16)
    dma = pltpu.SemaphoreType.DMA
    return pl.pallas_call(
        gather_kernel,
        out_shape=(
            heads_t(NX), heads_t(SLOTS), heads_t(SLOTS), heads_r(SLOTS), heads_r(SLOTS), heads_t(NX),
            jax.ShapeDtypeStruct((NX, BLK, D), BF16),
        ),
        in_specs=[VM] * 4 + [pl.BlockSpec(memory_space=pl.ANY)],
        out_specs=(VM,) * 7,
        scratch_shapes=[
            pltpu.VMEM((D, BLK), BF16),
            pltpu.VMEM((D, BLK), BF16),
            pltpu.VMEM((D, BLK), BF16),
            pltpu.VMEM((SLOTS, FEAT, BLK), BF16),
            pltpu.VMEM((SLOTS, FEAT, BLK), BF16),
            pltpu.VMEM((NX, FEAT, BLK), BF16),
            pltpu.VMEM((FEAT, D), BF16),
            dma((4, NX)),
            dma((4, NX)),
            dma((2, 2, NX)),
            dma((2, 2, NX)),
            dma,
        ],
        compiler_params=pltpu.CompilerParams(
            collective_id=0, has_side_effects=True, vmem_limit_bytes=40 * 2**20
        ),
        name="gather_heads",
    )(queries, keys, values, out_grad, out_weight)


def attend_kernel(
    len_ref, qt_ref, kt_ref, vt_ref, kr_ref, vr_ref, dt_ref, dy_ref,
    dq_out, dk_own, dv_own, dk_halo, dv_halo, wp_out,
    s_scr, p_scr, dq_acc, dk_acc, dv_acc, att_scr,
):
    z = lax.div(lax.axis_index("seq"), NX)
    first = (NX * z - REACH) * BLK
    dk_acc[...] = jnp.zeros_like(dk_acc)
    dv_acc[...] = jnp.zeros_like(dv_acc)

    ends = []
    total = jnp.int32(0)
    for i in range(NIMG):
        total = total + len_ref[0, i]
        ends.append(total)

    def bounds(pos):
        lo = jnp.zeros_like(pos)
        hi = jnp.full_like(pos, TOKENS)
        for e in ends:
            lo = jnp.where(e <= pos, e, lo)
        for e in reversed(ends):
            hi = jnp.where(e > pos, e, hi)
        return lo, hi

    def block(j, carry):
        base = (NX * z + j) * BLK
        lo_tok, _ = bounds(base)
        _, hi_tok = bounds(base + BLK - 1)
        k_lo = lax.div(lo_tok - first, BLK)
        k_hi = lax.div(hi_tok - first + BLK - 1, BLK)
        q_pos = base + lax.broadcasted_iota(jnp.int32, (8, BLK), 1)
        q_lo, q_hi = bounds(q_pos)
        q_lo, q_hi = q_lo[0:1], q_hi[0:1]
        rows = lax.broadcasted_iota(jnp.int32, (BLK, BLK), 0)

        def scores(kb, top):
            offset = first + kb * BLK
            keep = jnp.logical_and(rows >= q_lo - offset, rows < q_hi - offset)
            tops = []
            for h in range(HPD):
                s = dot_nn(kr_ref[h, kb], qt_ref[h, j]) * SCALE
                s = jnp.where(keep, s, NEG)
                s_scr[h, kb] = s
                tops.append(jnp.maximum(top[h], jnp.max(s, axis=0, keepdims=True)))
            return tuple(tops)

        top = lax.fori_loop(k_lo, k_hi, scores, (jnp.full((1, BLK), NEG, F32),) * HPD)

        def exps(kb, tot):
            out = []
            for h in range(HPD):
                e = jnp.exp(s_scr[h, kb] - top[h])
                s_scr[h, kb] = e
                out.append(tot[h] + jnp.sum(e, axis=0, keepdims=True))
            return tuple(out)

        norm = lax.fori_loop(k_lo, k_hi, exps, (jnp.zeros((1, BLK), F32),) * HPD)
        inv = [1.0 / n for n in norm]

        def mix(kb, acc):
            out = []
            for h in range(HPD):
                p = (s_scr[h, kb] * inv[h]).astype(BF16)
                p_scr[h, kb] = p
                out.append(acc[h] + dot_nn(vt_ref[h, kb], p))
            return tuple(out)

        mixed = lax.fori_loop(k_lo, k_hi, mix, (jnp.zeros((HD, BLK), F32),) * HPD)
        delta = []
        for h in range(HPD):
            att = mixed[h].astype(BF16)
            att_scr[h, j] = att
            delta.append(
                jnp.sum(dt_ref[h, j].astype(F32) * att.astype(F32), axis=0, keepdims=True)
            )

        def grads(kb, acc):
            out = []
            for h in range(HPD):
                feats = pl.ds(h * HD, HD)
                p = p_scr[h, kb]
                dp = dot_nn(vr_ref[h, kb], dt_ref[h, j])
                ds = (SCALE * p.astype(F32) * (dp - delta[h])).astype(BF16)
                out.append(acc[h] + dot_nn(kt_ref[h, kb], ds))
                dk_acc[kb, feats, :] += dot_nt(qt_ref[h, j], ds)
                dv_acc[kb, feats, :] += dot_nt(dt_ref[h, j], p)
            return tuple(out)

        dq = lax.fori_loop(k_lo, k_hi, grads, (jnp.zeros((HD, BLK), F32),) * HPD)
        for h in range(HPD):
            dq_acc[j, pl.ds(h * HD, HD), :] = dq[h]
        return carry

    lax.fori_loop(0, NX, block, 0)

    dq_out[...] = dq_acc[...].astype(BF16)
    for acc, own, halo in ((dk_acc, dk_own, dk_halo), (dv_acc, dv_own, dv_halo)):
        own[...] = acc[REACH : REACH + NX]
        halo[0:REACH] = acc[0:REACH].astype(BF16)
        halo[REACH:] = acc[REACH + NX :].astype(BF16)
    wp_out[...] = jnp.zeros_like(wp_out)
    for h in range(HPD):
        part = jnp.zeros((HD, D), F32)
        for j in range(NX):
            part = part + dot_nn(att_scr[h, j], dy_ref[j])
        wp_out[h, 0:HD, :] = part.astype(BF16)


def attend(lengths, qt, kt, vt, kr, vr, dt, dy):
    block = lambda n, dtype: jax.ShapeDtypeStruct((n, FEAT, BLK), dtype)
    return pl.pallas_call(
        attend_kernel,
        out_shape=(
            block(NX, BF16), block(NX, F32), block(NX, F32), block(2 * REACH, BF16),
            block(2 * REACH, BF16), jax.ShapeDtypeStruct((HPD, PADW, D), BF16),
        ),
        in_specs=[pl.BlockSpec(memory_space=pltpu.SMEM)] + [VM] * 7,
        out_specs=(VM,) * 6,
        scratch_shapes=[
            pltpu.VMEM((HPD, SLOTS, BLK, BLK), F32),
            pltpu.VMEM((HPD, SLOTS, BLK, BLK), BF16),
            pltpu.VMEM((NX, FEAT, BLK), F32),
            pltpu.VMEM((SLOTS, FEAT, BLK), F32),
            pltpu.VMEM((SLOTS, FEAT, BLK), F32),
            pltpu.VMEM((HPD, NX, HD, BLK), BF16),
        ],
        compiler_params=pltpu.CompilerParams(vmem_limit_bytes=48 * 2**20),
        name="attend",
    )(lengths, qt, kt, vt, kr, vr, dt, dy)


def return_kernel(
    dq_ref, dk_own, dv_own, dk_halo, dv_halo, wp_ref,
    gq_out, gk_out, gv_out, gw_out,
    rz_k, rz_v, t_k, t_v, rx_q, rx_k, rx_v, r1, s2, r2, tot, s3, r3,
    z_send, z_recv, x_send, x_recv, s1_send, s1_recv, s2_send, s2_recv, s3_send, s3_recv, l_sem,
):
    dp, z, x = place()
    seq = NX * z + x
    y, core = lax.div(dp, NCORE), lax.rem(dp, NCORE)
    up, down = lax.rem(z + 1, NZ), lax.rem(z + NZ - 1, NZ)
    barrier = pltpu.get_barrier_semaphore()
    reducer = z < NRED

    head = HPD * x + y
    owner = [2 * head, 2 * head + 1]
    my_head = lax.div(seq, 2)
    src_x, src_y = lax.div(my_head, HPD), lax.rem(my_head, HPD)
    half = lax.rem(seq, 2)

    def source(c, r):
        return (src_y * NCORE + c, NX * r + src_x)

    def is_source(c, r):
        return jnp.logical_and(
            jnp.logical_and(src_y * NCORE + c == dp, src_x == x), z == r
        )

    def is_me(t, d):
        return jnp.logical_and(owner[t] == seq, dp == d)

    for zz in (up, down):
        hello(barrier, (dp, NX * zz + x))
    for o in range(1, NX):
        hello(barrier, (dp, NX * z + lax.rem(x + o, NX)))
    for o in range(1, NDP):
        hello(barrier, (lax.rem(dp + o, NDP), seq))

    @pl.when(reducer)
    def _():
        for o in range(1, NZ):
            hello(barrier, (dp, NX * lax.rem(z + o, NZ) + x))

    for c in range(NCORE):
        for r in range(NRED):

            @pl.when(jnp.logical_not(is_source(c, r)))
            def _():
                hello(barrier, source(c, r))

    to_reducers = jnp.where(reducer, NRED - 1, NRED)
    mine_too = jnp.int32(0)
    for t in range(2):
        mine_too = mine_too + jnp.where(owner[t] == seq, 1, 0)
    to_owners = jnp.where(reducer, 2 * NDP - mine_too, 0)
    pl.semaphore_wait(barrier, 2 + NX - 1 + NDP - 1 + to_reducers + to_owners)

    def z_copy(t, halo, rz, side):
        zz = down if side == 0 else up
        return remote(
            halo.at[pl.ds(side * REACH, REACH)], rz.at[pl.ds(side * REACH, REACH)],
            z_send.at[t, side], z_recv.at[t, side], (dp, NX * zz + x),
        )

    kv = ((0, dk_halo, rz_k), (1, dv_halo, rz_v))
    for t, halo, rz in kv:
        for side in range(2):
            z_copy(t, halo, rz, side).start()

    def s1_copy(d):
        c = d % NCORE
        return remote(
            wp_ref.at[d // NCORE, :, pl.ds(CSTEP * c, CHUNK)], r1.at[dp],
            s1_send.at[d], s1_recv.at[dp], (jnp.int32(d), seq),
        )

    for d in range(NDP):

        @pl.when(d != dp)
        def _():
            s1_copy(d).start()

    def x_copy(t, src, rx, b):
        return remote(src.at[b], rx.at[x], x_send.at[t, b], x_recv.at[t, x], (dp, NX * z + b))

    def x_start(t, src, rx, b):
        @pl.when(b != x)
        def _():
            x_copy(t, src, rx, b).start()

        @pl.when(b == x)
        def _():
            rx[b] = src[b]

    def x_end(t, src, rx):
        for b in range(NX):

            @pl.when(b != x)
            def _():
                remote(
                    src.at[b], rx.at[b], x_send.at[t, b], x_recv.at[t, b], (dp, NX * z + b)
                ).wait_recv()

    def x_drain(t, src, rx):
        for b in range(NX):

            @pl.when(b != x)
            def _():
                x_copy(t, src, rx, b).wait_send()

    def give(rx, out):
        val = rx[...].astype(F32).reshape(D, BLK)
        for i in range(D // BLK):
            out[0, :, i * BLK : (i + 1) * BLK] = val[i * BLK : (i + 1) * BLK].T

    for b in range(NX):
        x_start(0, dq_ref, rx_q, b)

    for t, halo, rz, own, stage, rx in (
        (0, dk_halo, rz_k, dk_own, t_k, rx_k), (1, dv_halo, rz_v, dv_own, t_v, rx_v)
    ):
        for side in range(2):
            z_copy(t, halo, rz, side).wait_recv()
        for b in range(NX):
            val = own[b]
            if b >= 1:
                val = val + rz[b - 1].astype(F32)
            if b < REACH:
                val = val + rz[REACH + b].astype(F32)
            stage[b] = val.astype(BF16)
            x_start(1 + t, stage, rx, b)

    for d in range(NDP):

        @pl.when(d == dp)
        def _():
            r1[d] = wp_ref[d // NCORE, :, CSTEP * (d % NCORE) : CSTEP * (d % NCORE) + CHUNK]

    for d in range(NDP):

        @pl.when(d != dp)
        def _():
            remote(
                wp_ref.at[0, :, pl.ds(0, CHUNK)], r1.at[d], s1_send.at[d], s1_recv.at[d], (jnp.int32(d), seq)
            ).wait_recv()

    over_dp = r1[0].astype(F32)
    for d in range(1, NDP):
        over_dp = over_dp + r1[d].astype(F32)
    for r in range(NRED):
        s2[r] = over_dp[:, r * BLK : (r + 1) * BLK].astype(BF16)

    def s2_copy(r):
        return remote(s2.at[r], r2.at[z], s2_send.at[r], s2_recv.at[z], (dp, NX * r + x))

    for r in range(NRED):

        @pl.when(r != z)
        def _():
            s2_copy(r).start()

        @pl.when(r == z)
        def _():
            r2[r] = s2[r]

    x_end(0, dq_ref, rx_q)
    give(rx_q, gq_out)

    def s3_copy(t, d):
        return remote(
            s3.at[t], r3.at[core, z], s3_send.at[t, d], s3_recv.at[core, z], (jnp.int32(d), owner[t])
        )

    def s3_local(t):
        return pltpu.make_async_copy(s3.at[t], r3.at[core, z], l_sem)

    @pl.when(reducer)
    def _():
        for r in range(NZ):

            @pl.when(r != z)
            def _():
                remote(s2.at[0], r2.at[r], s2_send.at[0], s2_recv.at[r], (dp, NX * r + x)).wait_recv()

        over_z = r2[0].astype(F32)
        for r in range(1, NZ):
            over_z = over_z + r2[r].astype(F32)
        tot[...] = over_z * (ALL_TOK ** -0.5)
        s3[0] = tot[0:40, :]
        s3[1] = tot[ROWS : ROWS + 40, :]
        for t in range(2):
            for d in range(NDP):

                @pl.when(jnp.logical_not(is_me(t, d)))
                def _():
                    s3_copy(t, d).start()

                @pl.when(is_me(t, d))
                def _():
                    s3_local(t).start()

    x_end(1, t_k, rx_k)
    give(rx_k, gk_out)
    x_end(2, t_v, rx_v)
    give(rx_v, gv_out)

    for c in range(NCORE):
        for r in range(NRED):

            @pl.when(is_source(c, r))
            def _():
                pltpu.make_async_copy(s3.at[0], r3.at[c, r], l_sem).wait()

            @pl.when(jnp.logical_not(is_source(c, r)))
            def _():
                remote(
                    s3.at[0], r3.at[c, r], s3_send.at[0, 0], s3_recv.at[c, r], source(c, r)
                ).wait_recv()

            gw_out[:, c * CSTEP + r * BLK : c * CSTEP + (r + 1) * BLK] = r3[c, r, 0:ROWS, :]

    for t, halo, rz in kv:
        for side in range(2):
            z_copy(t, halo, rz, side).wait_send()
    for d in range(NDP):

        @pl.when(d != dp)
        def _():
            s1_copy(d).wait_send()

    x_drain(0, dq_ref, rx_q)
    x_drain(1, t_k, rx_k)
    x_drain(2, t_v, rx_v)
    for r in range(NRED):

        @pl.when(r != z)
        def _():
            s2_copy(r).wait_send()

    @pl.when(reducer)
    def _():
        for t in range(2):
            for d in range(NDP):

                @pl.when(jnp.logical_not(is_me(t, d)))
                def _():
                    s3_copy(t, d).wait_send()


def give_back(dq, dk_own, dv_own, dk_halo, dv_halo, wp):
    dma = pltpu.SemaphoreType.DMA
    grad = jax.ShapeDtypeStruct((1, BLK, D), F32)
    blocks = lambda n: pltpu.VMEM((n, FEAT, BLK), BF16)
    return pl.pallas_call(
        return_kernel,
        out_shape=(grad, grad, grad, jax.ShapeDtypeStruct((ROWS, D), F32)),
        in_specs=[VM] * 6,
        out_specs=(VM,) * 4,
        scratch_shapes=[
            blocks(2 * REACH), blocks(2 * REACH), blocks(NX), blocks(NX), blocks(NX), blocks(NX), blocks(NX),
            pltpu.VMEM((NDP, PADW, CHUNK), BF16),
            pltpu.VMEM((NRED, PADW, BLK), BF16),
            pltpu.VMEM((NZ, PADW, BLK), BF16),
            pltpu.VMEM((PADW, BLK), F32),
            pltpu.VMEM((2, 40, BLK), F32),
            pltpu.VMEM((NCORE, NRED, 40, BLK), F32),
            dma((2, 2)), dma((2, 2)), dma((3, NX)), dma((3, NX)),
            dma((NDP,)), dma((NDP,)), dma((NRED,)), dma((NZ,)), dma((2, NDP)), dma((NCORE, NRED)), dma,
        ],
        compiler_params=pltpu.CompilerParams(
            collective_id=1, has_side_effects=True, vmem_limit_bytes=40 * 2**20
        ),
        name="return_grads",
    )(dq, dk_own, dv_own, dk_halo, dv_halo, wp)


def body(queries, keys, values, out_weight, out_grad, lengths):
    qt, kt, vt, kr, vr, dt, dy = gather(queries, keys, values, out_grad, out_weight)
    grads = attend(lengths, qt, kt, vt, kr, vr, dt, dy)
    return give_back(*grads)


def solution(mesh):
    rows = P("dp", "seq", None)
    return jax.shard_map(
        body,
        mesh=mesh,
        in_specs=(rows, rows, rows, P(), rows, P("dp", None)),
        out_specs=(rows, rows, rows, P("seq", None)),
        check_vma=False,
    )
```

```python
import math

import jax
import jax.numpy as jnp
from jax import lax
from jax.experimental import pallas as pl
from jax.experimental.pallas import tpu as pltpu
from jax.sharding import PartitionSpec as P

NX, NZ = 4, 8
NY, NCORE = 4, 2
NDP = NY * NCORE
BLK = 128
HEADS, HD = 16, 72
HPD = HEADS // NX
FEAT = HPD * HD
D = HEADS * HD
REACH = 3
SLOTS = NX + 2 * REACH
WIDE = SLOTS * BLK
OWN = NX * BLK
NIMG = 20
TOKENS = 4096
ALL_TOK = 32768
SCALE = HD ** -0.5
LOG2E = math.log2(math.e)
NEG = -1e30
QG = 256
NG = OWN // QG
KG = QG + 2 * REACH * BLK
NCH = KG // BLK
PAIRS = HPD // 2
PF = 2 * HD
PADW = 80
CHUNK = 640
CSTEP = 512
NRED = 5
ROWS = D // (NX * NZ)
PADR = 48

F32, BF16 = jnp.float32, jnp.bfloat16
MESH = pl.DeviceIdType.MESH
VM = pl.BlockSpec(memory_space=pltpu.VMEM)
HB = pl.BlockSpec(memory_space=pltpu.HBM)


def remote(src, dst, send, recv, device):
    return pltpu.make_async_remote_copy(
        src_ref=src, dst_ref=dst, send_sem=send, recv_sem=recv, device_id=device, device_id_type=MESH
    )


def hello(barrier, device):
    pl.semaphore_signal(barrier, inc=1, device_id=device, device_id_type=MESH)


def dot_nn(a, b):
    return lax.dot_general(a, b, (((1,), (0,)), ((), ())), preferred_element_type=F32)


def dot_nt(a, b):
    return lax.dot_general(a, b, (((1,), (1,)), ((), ())), preferred_element_type=F32)


def main_kernel(
    len_ref, q_hbm, k_hbm, v_hbm, dy_hbm, w_hbm,
    rx_q, rx_k, rx_v, r3,
    kin, vin, qin, wbuf, dyw, ksend, vsend, qsend, kwin, vwin, qwin,
    qt, kt, vt, kr, vr, dt, s_scr, p_scr, ds_scr, att, dq_acc, dk_acc, dv_acc,
    dq_st, kh_st, vh_st, rz_k, rz_v, t_k, t_v,
    wp, r0, w1, r1, s2, r2, tot, s3,
    l_sem, x_send, x_recv, y_send, y_recv, f_send, f_recv, z_send, z_recv, g_send, g_recv,
    s0_send, s0_recv, s1_send, s1_recv, s2_send, s2_recv, s3_send, s3_recv, o_sem,
):
    dp, seq = lax.axis_index("dp"), lax.axis_index("seq")
    z, x = lax.div(seq, NX), lax.rem(seq, NX)
    y, core = lax.div(dp, NCORE), lax.rem(dp, NCORE)
    up, down = lax.rem(z + 1, NZ), lax.rem(z + NZ - 1, NZ)
    barrier = pltpu.get_barrier_semaphore()
    reducer = z < NRED
    order = (1, 3, 2)

    def xdev(o):
        return (dp, NX * z + lax.rem(x + o, NX))

    def zdev(zz):
        return (dp, NX * zz + x)

    def ydev(o):
        return (NCORE * lax.rem(y + o, NY) + core, seq)

    twin = (dp + 1 - 2 * core, seq)

    loads = [
        pltpu.make_async_copy(k_hbm.at[0], kin, l_sem.at[0]),
        pltpu.make_async_copy(v_hbm.at[0], vin, l_sem.at[1]),
        pltpu.make_async_copy(q_hbm.at[0], qin, l_sem.at[2]),
        pltpu.make_async_copy(dy_hbm.at[0], dyw.at[x], l_sem.at[3]),
        pltpu.make_async_copy(w_hbm.at[pl.ds(pl.multiple_of(FEAT * x, 32), FEAT)], wbuf, l_sem.at[4]),
    ]
    for copy in loads:
        copy.start()

    head = HPD * x + y
    owner = [2 * head, 2 * head + 1]
    my_head = lax.div(seq, 2)
    src_x, src_y = lax.div(my_head, HPD), lax.rem(my_head, HPD)

    def source(c, r):
        return (src_y * NCORE + c, NX * r + src_x)

    def is_source(c, r):
        return jnp.logical_and(jnp.logical_and(src_y * NCORE + c == dp, src_x == x), z == r)

    def is_me(t, d):
        return jnp.logical_and(owner[t] == seq, dp == d)

    for o in order:
        hello(barrier, xdev(o))
    for zz in (up, down):
        hello(barrier, zdev(zz))
    hello(barrier, twin)
    for o in order:
        hello(barrier, ydev(o))

    @pl.when(reducer)
    def _():
        for o in range(1, NZ):
            hello(barrier, zdev(lax.rem(z + o, NZ)))

    for c in range(NCORE):
        for r in range(NRED):

            @pl.when(jnp.logical_not(is_source(c, r)))
            def _():
                hello(barrier, source(c, r))

    to_reducers = jnp.where(reducer, NRED - 1, NRED)
    mine_too = jnp.int32(0)
    for t in range(2):
        mine_too = mine_too + jnp.where(owner[t] == seq, 1, 0)
    to_owners = jnp.where(reducer, 2 * NDP - mine_too, 0)

    def turn(src, dst):
        for i in range(D // BLK):
            tile = src[:, i * BLK : (i + 1) * BLK].astype(F32)
            dst[i * BLK : (i + 1) * BLK, :] = tile.T.astype(BF16)

    def part(ref, xp):
        return ref.at[pl.ds(pl.multiple_of(FEAT * xp, 32), FEAT)]

    def x_copy(t, o, src, win, base):
        xp = lax.rem(x + o, NX)
        return remote(part(src, xp), win.at[base + x], x_send.at[t, o], x_recv.at[t, NX - o], xdev(o))

    def x_wait(t, o, src, win, base):
        xp = lax.rem(x + o, NX)
        remote(part(src, xp), win.at[base + xp], x_send.at[t, o], x_recv.at[t, o], xdev(o)).wait_recv()

    def y_copy(o):
        return remote(dyw.at[x], dyw.at[x], y_send.at[o], y_recv.at[NX - o], xdev(o))

    def y_wait(o):
        xp = lax.rem(x + o, NX)
        remote(dyw.at[x], dyw.at[xp], y_send.at[o], y_recv.at[o], xdev(o)).wait_recv()

    def y_relay():
        xp = lax.rem(x + NX - RELAY, NX)
        return remote(dyw.at[xp], dyw.at[xp], y_send.at[2], y_recv.at[2], xdev(RELAY))

    mine = pl.ds(pl.multiple_of(FEAT * x, 32), FEAT)
    loads[0].wait()
    turn(kin, ksend)
    pl.semaphore_wait(barrier, 2 * (NX - 1) + 3 + to_reducers + to_owners)
    for o in order:
        x_copy(0, o, ksend, kwin, REACH).start()
    loads[1].wait()
    turn(vin, vsend)
    for o in order:
        x_copy(1, o, vsend, vwin, REACH).start()
    loads[2].wait()
    turn(qin, qsend)
    for o in order:
        x_copy(2, o, qsend, qwin, 0).start()
    loads[3].wait()
    for o in (NX - RELAY, RELAY)[::-1]:
        y_copy(o).start()
    kwin[REACH + x] = ksend[mine, :]
    vwin[REACH + x] = vsend[mine, :]
    qwin[x] = qsend[mine, :]

    def z_up(t, xp, win):
        return remote(
            win.at[REACH + xp], win.at[xp + NX + REACH], f_send.at[t, 0, xp], f_recv.at[t, 0, xp], zdev(down)
        )

    def z_down(t, xp, win):
        return remote(win.at[REACH + xp], win.at[xp - 1], f_send.at[t, 1, xp], f_recv.at[t, 1, xp], zdev(up))

    for t, src, win in ((0, ksend, kwin), (1, vsend, vwin)):
        for o in (0,) + order:
            xp = lax.rem(x + o, NX)
            if o:
                x_wait(t, o, src, win, REACH)

            @pl.when(xp < REACH)
            def _():
                z_up(t, xp, win).start()

            @pl.when(xp >= 1)
            def _():
                z_down(t, xp, win).start()

    def unpack(win, slot, t_out, r_out):
        val = win[slot].astype(F32)
        cols = pl.ds(pl.multiple_of(slot * BLK, BLK), BLK)
        for h in range(HPD):
            piece = val[h * HD : (h + 1) * HD]
            t_out[h, :, cols] = piece.astype(BF16)
            if r_out is not None:
                r_out[h, cols, :] = piece.T.astype(BF16)

    def unpack_kv(slot, carry):
        unpack(kwin, slot, kt, kr)
        unpack(vwin, slot, vt, vr)
        return carry

    def unpack_q(slot, carry):
        unpack(qwin, slot, qt, None)
        return carry

    lax.fori_loop(REACH, REACH + NX, unpack_kv, 0)
    for o in order:
        x_wait(2, o, qsend, qwin, 0)
    lax.fori_loop(0, NX, unpack_q, 0)
    for t, win in ((0, kwin), (1, vwin)):
        for xp in range(REACH):
            z_up(t, xp, win).wait_recv()
            z_down(t, xp + 1, win).wait_recv()
    lax.fori_loop(0, REACH, unpack_kv, 0)
    lax.fori_loop(REACH + NX, SLOTS, unpack_kv, 0)
    y_wait(NX - RELAY)
    y_relay().start()

    first = (NX * z - REACH) * BLK
    rows = lax.broadcasted_iota(jnp.int32, (BLK, QG), 0)
    ends = []
    total = jnp.int32(0)
    for i in range(NIMG):
        total = total + len_ref[0, i]
        ends.append(total)

    spans = []
    for g in range(NG):
        pos = NX * z * BLK + g * QG + lax.broadcasted_iota(jnp.int32, (8, QG), 1)
        lo = jnp.zeros_like(pos)
        hi = jnp.full_like(pos, TOKENS)
        for e in ends:
            lo = jnp.where(e <= pos, e, lo)
        for e in ends[::-1]:
            hi = jnp.where(e > pos, e, hi)
        spans.append((lo[0:1] - first - g * QG, hi[0:1] - first - g * QG))

    def forward(h, carry):
        for g in range(NG):
            lo, hi = spans[g]
            q_blk = qt[h, :, g * QG : (g + 1) * QG]
            top = jnp.full((1, QG), NEG, F32)
            for c in range(NCH):
                keys = slice(g * QG + c * BLK, g * QG + (c + 1) * BLK)
                s = dot_nn(kr[h, keys, :], q_blk)
                keep = jnp.logical_and(rows >= lo - c * BLK, rows < hi - c * BLK)
                s = jnp.where(keep, s, NEG)
                s_scr[g, c * BLK : (c + 1) * BLK, :] = s
                top = jnp.maximum(top, jnp.max(s, axis=0, keepdims=True))
            norm = jnp.zeros((1, QG), F32)
            for c in range(NCH):
                e = jnp.exp2((s_scr[g, c * BLK : (c + 1) * BLK, :] - top) * (SCALE * LOG2E))
                s_scr[g, c * BLK : (c + 1) * BLK, :] = e
                norm = norm + jnp.sum(e, axis=0, keepdims=True)
            inv = 1.0 / norm
            for c in range(NCH):
                p_scr[g, h, c * BLK : (c + 1) * BLK, :] = (
                    s_scr[g, c * BLK : (c + 1) * BLK, :] * inv
                ).astype(BF16)
            mixed = dot_nn(vt[h, :, g * QG : g * QG + KG], p_scr[g, h])
            att[h, :, g * QG : (g + 1) * QG] = mixed.astype(BF16)
        return carry

    lax.fori_loop(0, HPD, forward, 0)

    loads[4].wait()
    y_wait(RELAY)
    xp2 = lax.rem(x + 2, NX)
    remote(dyw.at[xp2], dyw.at[xp2], y_send.at[2], y_recv.at[2], xdev(RELAY)).wait_recv()
    for b in range(NX):
        d_blk = dot_nt(wbuf[...], dyw[b])
        for h in range(HPD):
            dt[h, :, b * BLK : (b + 1) * BLK] = d_blk[h * HD : (h + 1) * HD].astype(BF16)
    wp[...] = jnp.zeros_like(wp)
    dy_all = dyw[...].reshape(OWN, D)
    for h in range(HPD):
        wp[h, 0:HD, :] = dot_nn(att[h], dy_all).astype(BF16)

    far = pl.ds(pl.multiple_of(CSTEP * (1 - core), BLK), CHUNK)
    near = pl.ds(pl.multiple_of(CSTEP * core, BLK), CHUNK)
    s0_copy = remote(wp.at[:, :, far], r0, s0_send, s0_recv, twin)
    s0_copy.start()

    def s1_copy(o):
        return remote(
            w1.at[lax.rem(y + o, NY)], r1.at[NY - o], s1_send.at[o], s1_recv.at[NY - o], ydev(o)
        )

    def s1_begin():
        s0_copy.wait_recv()
        for h in range(HPD):
            w1[h] = (wp[h, :, near].astype(F32) + r0[h].astype(F32)).astype(BF16)
        for o in order:
            s1_copy(o).start()

    def s2_copy(r):
        return remote(s2.at[r], r2.at[z], s2_send.at[r], s2_recv.at[z], (dp, NX * r + x))

    def s2_begin():
        over_dp = w1[y].astype(F32)
        for o in order:
            remote(w1.at[0], r1.at[o], s1_send.at[o], s1_recv.at[o], ydev(o)).wait_recv()
            over_dp = over_dp + r1[o].astype(F32)
        for r in range(NRED):
            s2[r] = over_dp[:, r * BLK : (r + 1) * BLK].astype(BF16)
        for r in range(NRED):

            @pl.when(r != z)
            def _():
                s2_copy(r).start()

            @pl.when(r == z)
            def _():
                r2[r] = s2[r]

    def s3_copy(t, d):
        return remote(
            s3.at[t], r3.at[core, z], s3_send.at[t, d], s3_recv.at[core, z], (jnp.int32(d), owner[t])
        )

    def s3_begin():
        @pl.when(reducer)
        def _():
            for r in range(NZ):

                @pl.when(r != z)
                def _():
                    remote(s2.at[0], r2.at[r], s2_send.at[0], s2_recv.at[r], (dp, NX * r + x)).wait_recv()

            over_z = r2[0].astype(F32)
            for r in range(1, NZ):
                over_z = over_z + r2[r].astype(F32)
            tot[0:PADW, :] = over_z * (ALL_TOK ** -0.5)
            tot[PADW:, :] = jnp.zeros((8, BLK), F32)
            for t in range(2):
                s3[t] = tot[t * ROWS : t * ROWS + PADR, :].astype(BF16)
            for t in range(2):
                for d in range(NDP):

                    @pl.when(jnp.logical_not(is_me(t, d)))
                    def _():
                        s3_copy(t, d).start()

                    @pl.when(is_me(t, d))
                    def _():
                        pltpu.make_async_copy(s3.at[t], r3.at[core, z], o_sem).start()

    def backward(h, i, pair):
        feats = slice(i * HD, (i + 1) * HD)
        for g in range(NG):
            cols = slice(g * QG, (g + 1) * QG)
            q_blk, d_blk, p_all = qt[h, :, cols], dt[h, :, cols], p_scr[g, h]
            delta = jnp.sum(d_blk.astype(F32) * att[h, :, cols].astype(F32), axis=0, keepdims=True)
            for c in range(NCH):
                keys = slice(g * QG + c * BLK, g * QG + (c + 1) * BLK)
                dp_c = dot_nn(vr[h, keys, :], d_blk)
                p = p_scr[g, h, c * BLK : (c + 1) * BLK, :].astype(F32)
                ds_scr[g, c * BLK : (c + 1) * BLK, :] = (SCALE * p * (dp_c - delta)).astype(BF16)
            ds = ds_scr[g]
            dq_acc[pair, feats, cols] = dot_nn(kt[h, :, g * QG : g * QG + KG], ds)
            for acc, left, right in ((dk_acc, q_blk, ds), (dv_acc, d_blk, p_all)):
                add = dot_nt(left, right)
                if g == 0:
                    acc[pair, feats, 0:KG] = add
                else:
                    old = g * QG + KG - QG
                    acc[pair, feats, g * QG : old] += add[:, 0 : KG - QG]
                    acc[pair, feats, old : old + QG] = add[:, KG - QG :]

    def z_copy(t, p, side):
        stage, rz = ((kh_st, rz_k), (vh_st, rz_v))[t]
        zz = down if side == 0 else up
        slots = pl.ds(side * REACH, REACH)
        return remote(
            stage.at[p, slots], rz.at[p, slots], z_send.at[t, p, side], z_recv.at[t, p, side], zdev(zz)
        )

    returns = ((dq_st, rx_q), (t_k, rx_k), (t_v, rx_v))

    def g_copy(t, p, b):
        stage, rx = returns[t]
        return remote(
            stage.at[p, b], rx.at[x, pl.ds(PF * p, PF)], g_send.at[t, p, b], g_recv.at[t, p, x], (dp, NX * z + b)
        )

    def g_start(t, p, b):
        stage, rx = returns[t]

        @pl.when(b != x)
        def _():
            g_copy(t, p, b).start()

        @pl.when(b == x)
        def _():
            rx[b, PF * p : PF * (p + 1), :] = stage[p, b]

    def g_wait(t, p):
        stage, rx = returns[t]
        for b in range(NX):

            @pl.when(b != x)
            def _():
                remote(
                    stage.at[p, b], rx.at[b, pl.ds(PF * p, PF)], g_send.at[t, p, b], g_recv.at[t, p, b],
                    (dp, NX * z + b),
                ).wait_recv()

    def halo_send(p):
        for t, acc, stage in ((0, dk_acc, kh_st), (1, dv_acc, vh_st)):
            for side in range(2):
                for i in range(REACH):
                    slot = i + side * (NX + REACH)
                    stage[p, side * REACH + i] = acc[p, :, slot * BLK : (slot + 1) * BLK].astype(BF16)
                z_copy(t, p, side).start()
        for b in range(NX):
            dq_st[p, b] = dq_acc[p, :, b * BLK : (b + 1) * BLK].astype(BF16)
            g_start(0, p, b)

    def halo_add(p):
        for t, acc, rz in ((0, dk_acc, rz_k), (1, dv_acc, rz_v)):
            for side in range(2):
                z_copy(t, p, side).wait_recv()
            stage = returns[1 + t][0]
            for b in range(NX):
                val = acc[p, :, (REACH + b) * BLK : (REACH + b + 1) * BLK]
                if b >= 1:
                    val = val + rz[p, b - 1].astype(F32)
                if b < REACH:
                    val = val + rz[p, REACH + b].astype(F32)
                stage[p, b] = val.astype(BF16)
                g_start(1 + t, p, b)

    backward(0, 0, 0)
    s1_begin()
    backward(1, 1, 0)
    halo_send(0)
    backward(2, 0, 1)
    backward(3, 1, 1)
    halo_send(1)
    s2_begin()
    halo_add(0)
    s3_begin()
    halo_add(1)

    for c in range(NCORE):
        for r in range(NRED):

            @pl.when(is_source(c, r))
            def _():
                pltpu.make_async_copy(s3.at[0], r3.at[c, r], o_sem).wait()

            @pl.when(jnp.logical_not(is_source(c, r)))
            def _():
                remote(s3.at[0], r3.at[c, r], s3_send.at[0, 0], s3_recv.at[c, r], source(c, r)).wait_recv()

    for t in range(3):
        for p in range(PAIRS):
            g_wait(t, p)
    for o in order:
        x_copy(0, o, ksend, kwin, REACH).wait_send()
        x_copy(1, o, vsend, vwin, REACH).wait_send()
        x_copy(2, o, qsend, qwin, 0).wait_send()
    y_copy(RELAY).wait_send()
    y_copy(NX - RELAY).wait_send()
    y_relay().wait_send()
    for t, win in ((0, kwin), (1, vwin)):
        for xp in range(REACH):
            z_up(t, xp, win).wait_send()
            z_down(t, xp + 1, win).wait_send()
    for t in range(2):
        for p in range(PAIRS):
            for side in range(2):
                z_copy(t, p, side).wait_send()
    for t in range(3):
        for p in range(PAIRS):
            for b in range(NX):

                @pl.when(b != x)
                def _():
                    g_copy(t, p, b).wait_send()

    s0_copy.wait_send()
    for o in order:
        s1_copy(o).wait_send()
    for r in range(NRED):

        @pl.when(r != z)
        def _():
            s2_copy(r).wait_send()

    @pl.when(reducer)
    def _():
        for t in range(2):
            for d in range(NDP):

                @pl.when(jnp.logical_not(is_me(t, d)))
                def _():
                    s3_copy(t, d).wait_send()


RELAY = NX - 1


def main_call(lengths, queries, keys, values, out_grad, out_weight):
    dma = pltpu.SemaphoreType.DMA
    b16 = lambda *shape: pltpu.VMEM(shape, BF16)
    f32 = lambda *shape: pltpu.VMEM(shape, F32)
    back = jax.ShapeDtypeStruct((NX, FEAT, BLK), BF16)
    return pl.pallas_call(
        main_kernel,
        out_shape=(back, back, back, jax.ShapeDtypeStruct((NCORE, NRED, PADR, BLK), BF16)),
        in_specs=[pl.BlockSpec(memory_space=pltpu.SMEM)] + [HB] * 5,
        out_specs=(VM,) * 4,
        scratch_shapes=[
            b16(BLK, D), b16(BLK, D), b16(BLK, D), b16(FEAT, D), b16(NX, BLK, D),
            b16(D, BLK), b16(D, BLK), b16(D, BLK),
            b16(SLOTS, FEAT, BLK), b16(SLOTS, FEAT, BLK), b16(NX, FEAT, BLK),
            b16(HPD, HD, OWN), b16(HPD, HD, WIDE), b16(HPD, HD, WIDE), b16(HPD, WIDE, HD), b16(HPD, WIDE, HD),
            b16(HPD, HD, OWN),
            f32(NG, KG, QG), b16(NG, HPD, KG, QG), b16(NG, KG, QG), b16(HPD, HD, OWN),
            f32(PAIRS, PF, OWN), f32(PAIRS, PF, WIDE), f32(PAIRS, PF, WIDE),
            b16(PAIRS, NX, PF, BLK), b16(PAIRS, 2 * REACH, PF, BLK), b16(PAIRS, 2 * REACH, PF, BLK),
            b16(PAIRS, 2 * REACH, PF, BLK), b16(PAIRS, 2 * REACH, PF, BLK),
            b16(PAIRS, NX, PF, BLK), b16(PAIRS, NX, PF, BLK),
            b16(HPD, PADW, D), b16(HPD, PADW, CHUNK), b16(HPD, PADW, CHUNK), b16(NY, PADW, CHUNK),
            b16(NRED, PADW, BLK), b16(NZ, PADW, BLK), f32(PADW + 8, BLK), b16(2, PADR, BLK),
            dma((5,)), dma((3, NX)), dma((3, NX)), dma((NX,)), dma((NX,)), dma((2, 2, NX)), dma((2, 2, NX)),
            dma((2, PAIRS, 2)), dma((2, PAIRS, 2)), dma((3, PAIRS, NX)), dma((3, PAIRS, NX)),
            dma, dma, dma((NY,)), dma((NY,)), dma((NRED,)), dma((NZ,)), dma((2, NDP)), dma((NCORE, NRED)), dma,
        ],
        compiler_params=pltpu.CompilerParams(
            collective_id=0, has_side_effects=True, vmem_limit_bytes=52 * 2**20
        ),
        name="attention_backward",
    )(lengths, queries, keys, values, out_grad, out_weight)


PART = 3 * BLK


def finish_kernel(rq, rk, rv, rw, gq, gk, gv, gw):
    for src, dst in ((rq, gq), (rk, gk), (rv, gv)):
        for i in range(PART // BLK):
            tile = src[i * BLK : (i + 1) * BLK, :].astype(F32)
            dst[0, :, i * BLK : (i + 1) * BLK] = tile.T

    @pl.when(pl.program_id(0) == 0)
    def _():
        for c in range(NCORE):
            for r in range(NRED):
                col = c * CSTEP + r * BLK
                gw[:, col : col + BLK] = rw[c, r, 0:ROWS, :].astype(F32)


def finish(rq, rk, rv, rw):
    grad = jax.ShapeDtypeStruct((1, BLK, D), F32)
    wide = pl.BlockSpec((PART, BLK), lambda i: (i, 0))
    tall = pl.BlockSpec((1, BLK, PART), lambda i: (0, 0, i))
    return pl.pallas_call(
        finish_kernel,
        grid=(D // PART,),
        out_shape=(grad, grad, grad, jax.ShapeDtypeStruct((ROWS, D), F32)),
        in_specs=[wide] * 3 + [pl.BlockSpec((NCORE, NRED, PADR, BLK), lambda i: (0, 0, 0, 0))],
        out_specs=(tall, tall, tall, pl.BlockSpec((ROWS, D), lambda i: (0, 0))),
        name="outputs",
    )(*[r.reshape(D, BLK) for r in (rq, rk, rv)], rw)


def body(queries, keys, values, out_weight, out_grad, lengths):
    return finish(*main_call(lengths, queries, keys, values, out_grad, out_weight))


def solution(mesh):
    rows = P("dp", "seq", None)
    return jax.shard_map(
        body,
        mesh=mesh,
        in_specs=(rows, rows, rows, P(), rows, P("dp", None)),
        out_specs=(rows, rows, rows, P("seq", None)),
        check_vma=False,
    )
```

```python
import math

import jax
import jax.numpy as jnp
from jax import lax
from jax.experimental import pallas as pl
from jax.experimental.pallas import tpu as pltpu
from jax.sharding import PartitionSpec as P

NX, NZ = 4, 8
NY, NCORE = 4, 2
NDP = NY * NCORE
BLK = 128
HEADS, HD = 16, 72
HPD = HEADS // NX
FEAT = HPD * HD
D = HEADS * HD
REACH = 3
SLOTS = NX + 2 * REACH
WIDE = SLOTS * BLK
OWN = NX * BLK
NIMG = 20
TOKENS = 4096
ALL_TOK = 32768
SCALE = HD ** -0.5
LOG2E = math.log2(math.e)
NEG = -1e30
QG = 256
NG = OWN // QG
KG = QG + 2 * REACH * BLK
NCH = KG // BLK
PAIRS = HPD // 2
PF = 2 * HD
PADW = 80
CHUNK = 640
CSTEP = 512
NRED = 5
ROWS = D // (NX * NZ)
PADR = 48

F32, BF16 = jnp.float32, jnp.bfloat16
MESH = pl.DeviceIdType.MESH
VM = pl.BlockSpec(memory_space=pltpu.VMEM)
HB = pl.BlockSpec(memory_space=pltpu.HBM)


def remote(src, dst, send, recv, device):
    return pltpu.make_async_remote_copy(
        src_ref=src, dst_ref=dst, send_sem=send, recv_sem=recv, device_id=device, device_id_type=MESH
    )


def hello(barrier, device):
    pl.semaphore_signal(barrier, inc=1, device_id=device, device_id_type=MESH)


def dot_nn(a, b):
    return lax.dot_general(a, b, (((1,), (0,)), ((), ())), preferred_element_type=F32)


def dot_nt(a, b):
    return lax.dot_general(a, b, (((1,), (1,)), ((), ())), preferred_element_type=F32)


def main_kernel(
    len_ref, q_hbm, k_hbm, v_hbm, dy_hbm, w_hbm,
    rx_q, rx_k, rx_v, r3,
    kin, vin, qin, wbuf, dyw, ksend, vsend, qsend, kwin, vwin, qwin,
    qt, kt, vt, kr, vr, dt, s_scr, p_scr, ds_scr, att, dq_acc, dk_acc, dv_acc,
    dq_st, kh_st, vh_st, rz_k, rz_v, t_k, t_v,
    wp, r0, w1, r1, s2, r2, tot, s3, h5,
    l_sem, x_send, x_recv, y_send, y_recv, f_send, f_recv, z_send, z_recv, g_send, g_recv,
    s0_send, s0_recv, s1_send, s1_recv, s2_send, s2_recv, s3_send, s3_recv, s4_send, s4_recv, s5_send, s5_recv,
):
    dp, seq = lax.axis_index("dp"), lax.axis_index("seq")
    z, x = lax.div(seq, NX), lax.rem(seq, NX)
    y, core = lax.div(dp, NCORE), lax.rem(dp, NCORE)
    up, down = lax.rem(z + 1, NZ), lax.rem(z + NZ - 1, NZ)
    barrier = pltpu.get_barrier_semaphore()
    reducer = z < NRED
    order = (1, 3, 2)

    def xdev(o):
        return (dp, NX * z + lax.rem(x + o, NX))

    def zdev(zz):
        return (dp, NX * zz + x)

    def ydev(o):
        return (NCORE * lax.rem(y + o, NY) + core, seq)

    twin = (dp + 1 - 2 * core, seq)

    loads = [
        pltpu.make_async_copy(k_hbm.at[0], kin, l_sem.at[0]),
        pltpu.make_async_copy(v_hbm.at[0], vin, l_sem.at[1]),
        pltpu.make_async_copy(q_hbm.at[0], qin, l_sem.at[2]),
        pltpu.make_async_copy(dy_hbm.at[0], dyw.at[x], l_sem.at[3]),
        pltpu.make_async_copy(w_hbm.at[pl.ds(pl.multiple_of(FEAT * x, 32), FEAT)], wbuf, l_sem.at[4]),
    ]
    for copy in loads:
        copy.start()

    head = HPD * x + y
    owner = [2 * head, 2 * head + 1]
    my_head = lax.div(seq, 2)
    src_x, src_y = lax.div(my_head, HPD), lax.rem(my_head, HPD)
    collector = src_y == y

    def is_source(r):
        return jnp.logical_and(src_x == x, z == r)

    for o in order:
        hello(barrier, xdev(o))
    for zz in (up, down):
        hello(barrier, zdev(zz))
    hello(barrier, twin)
    for o in order:
        hello(barrier, ydev(o))

    @pl.when(reducer)
    def _():
        for o in range(1, NZ):
            hello(barrier, zdev(lax.rem(z + o, NZ)))

    for r in range(NRED):

        @pl.when(jnp.logical_and(collector, jnp.logical_not(is_source(r))))
        def _():
            hello(barrier, (dp, NX * r + src_x))

    to_reducers = jnp.where(reducer, NRED - 1, NRED)
    mine_too = jnp.int32(0)
    for t in range(2):
        mine_too = mine_too + jnp.where(owner[t] == seq, 1, 0)
    to_owners = jnp.where(reducer, 2 - mine_too, 0)

    def turn(src, dst):
        for i in range(D // BLK):
            tile = src[:, i * BLK : (i + 1) * BLK].astype(F32)
            dst[i * BLK : (i + 1) * BLK, :] = tile.T.astype(BF16)

    def part(ref, xp):
        return ref.at[pl.ds(pl.multiple_of(FEAT * xp, 32), FEAT)]

    def x_copy(t, o, src, win, base):
        xp = lax.rem(x + o, NX)
        return remote(part(src, xp), win.at[base + x], x_send.at[t, o], x_recv.at[t, NX - o], xdev(o))

    def x_wait(t, o, src, win, base):
        xp = lax.rem(x + o, NX)
        remote(part(src, xp), win.at[base + xp], x_send.at[t, o], x_recv.at[t, o], xdev(o)).wait_recv()

    def y_copy(o):
        return remote(dyw.at[x], dyw.at[x], y_send.at[o // 2], y_recv.at[(NX - o) // 2], xdev(o))

    def y_wait(o):
        xp = lax.rem(x + o, NX)
        remote(dyw.at[x], dyw.at[xp], y_send.at[o // 2], y_recv.at[o // 2], xdev(o)).wait_recv()

    def y_relay(o):
        block = dyw.at[lax.rem(x + o, NX), pl.ds(o // 2 * (BLK // 2), BLK // 2)]
        return remote(block, block, y_send.at[2 + o // 2], y_recv.at[2 + o // 2], xdev(NX - o))

    def y_relay_wait(o):
        block = dyw.at[lax.rem(x + 2, NX), pl.ds(o // 2 * (BLK // 2), BLK // 2)]
        remote(block, block, y_send.at[2 + o // 2], y_recv.at[2 + o // 2], xdev(NX - o)).wait_recv()

    mine = pl.ds(pl.multiple_of(FEAT * x, 32), FEAT)
    loads[0].wait()
    turn(kin, ksend)
    pl.semaphore_wait(barrier, 2 * (NX - 1) + 3 + to_reducers + to_owners)
    for o in order:
        x_copy(0, o, ksend, kwin, REACH).start()
    loads[1].wait()
    turn(vin, vsend)
    for o in order:
        x_copy(1, o, vsend, vwin, REACH).start()
    loads[2].wait()
    turn(qin, qsend)
    for o in order:
        x_copy(2, o, qsend, qwin, 0).start()
    loads[3].wait()
    for o in (1, 3):
        y_copy(o).start()
    kwin[REACH + x] = ksend[mine, :]
    vwin[REACH + x] = vsend[mine, :]
    qwin[x] = qsend[mine, :]

    def z_up(t, xp, win):
        return remote(
            win.at[REACH + xp], win.at[xp + NX + REACH], f_send.at[t, 0, xp], f_recv.at[t, 0, xp], zdev(down)
        )

    def z_down(t, xp, win):
        return remote(win.at[REACH + xp], win.at[xp - 1], f_send.at[t, 1, xp], f_recv.at[t, 1, xp], zdev(up))

    for t, src, win in ((0, ksend, kwin), (1, vsend, vwin)):
        for o in (0,) + order:
            xp = lax.rem(x + o, NX)
            if o:
                x_wait(t, o, src, win, REACH)

            @pl.when(xp < REACH)
            def _():
                z_up(t, xp, win).start()

            @pl.when(xp >= 1)
            def _():
                z_down(t, xp, win).start()

    def unpack(win, slot, t_out, r_out):
        val = win[slot].astype(F32)
        cols = pl.ds(pl.multiple_of(slot * BLK, BLK), BLK)
        for h in range(HPD):
            piece = val[h * HD : (h + 1) * HD]
            t_out[h, :, cols] = piece.astype(BF16)
            if r_out is not None:
                r_out[h, cols, :] = piece.T.astype(BF16)

    def unpack_kv(slot, carry):
        unpack(kwin, slot, kt, kr)
        unpack(vwin, slot, vt, vr)
        return carry

    def unpack_q(slot, carry):
        unpack(qwin, slot, qt, None)
        return carry

    lax.fori_loop(REACH, REACH + NX, unpack_kv, 0)
    for o in order:
        x_wait(2, o, qsend, qwin, 0)
    lax.fori_loop(0, NX, unpack_q, 0)
    for t, win in ((0, kwin), (1, vwin)):
        for xp in range(REACH):
            z_up(t, xp, win).wait_recv()
            z_down(t, xp + 1, win).wait_recv()
    lax.fori_loop(0, REACH, unpack_kv, 0)
    lax.fori_loop(REACH + NX, SLOTS, unpack_kv, 0)
    for o in (1, 3):
        y_wait(o)
        y_relay(o).start()

    first = (NX * z - REACH) * BLK
    rows = lax.broadcasted_iota(jnp.int32, (BLK, QG), 0)
    ends = []
    total = jnp.int32(0)
    for i in range(NIMG):
        total = total + len_ref[0, i]
        ends.append(total)

    spans = []
    for g in range(NG):
        pos = NX * z * BLK + g * QG + lax.broadcasted_iota(jnp.int32, (8, QG), 1)
        lo = jnp.zeros_like(pos)
        hi = jnp.full_like(pos, TOKENS)
        for e in ends:
            lo = jnp.where(e <= pos, e, lo)
        for e in ends[::-1]:
            hi = jnp.where(e > pos, e, hi)
        spans.append((lo[0:1] - first - g * QG, hi[0:1] - first - g * QG))

    def forward(h, carry):
        for g in range(NG):
            lo, hi = spans[g]
            q_blk = qt[h, :, g * QG : (g + 1) * QG]
            top = jnp.full((1, QG), NEG, F32)
            for c in range(NCH):
                keys = slice(g * QG + c * BLK, g * QG + (c + 1) * BLK)
                s = dot_nn(kr[h, keys, :], q_blk)
                keep = jnp.logical_and(rows >= lo - c * BLK, rows < hi - c * BLK)
                s = jnp.where(keep, s, NEG)
                s_scr[g, c * BLK : (c + 1) * BLK, :] = s
                top = jnp.maximum(top, jnp.max(s, axis=0, keepdims=True))
            norm = jnp.zeros((1, QG), F32)
            for c in range(NCH):
                e = jnp.exp2((s_scr[g, c * BLK : (c + 1) * BLK, :] - top) * (SCALE * LOG2E))
                s_scr[g, c * BLK : (c + 1) * BLK, :] = e
                norm = norm + jnp.sum(e, axis=0, keepdims=True)
            inv = 1.0 / norm
            for c in range(NCH):
                p_scr[g, h, c * BLK : (c + 1) * BLK, :] = (
                    s_scr[g, c * BLK : (c + 1) * BLK, :] * inv
                ).astype(BF16)
            mixed = dot_nn(vt[h, :, g * QG : g * QG + KG], p_scr[g, h])
            att[h, :, g * QG : (g + 1) * QG] = mixed.astype(BF16)
        return carry

    far = pl.ds(pl.multiple_of(CSTEP * (1 - core), BLK), CHUNK)
    near = pl.ds(pl.multiple_of(CSTEP * core, BLK), CHUNK)
    s0_copy = remote(wp.at[:, :, far], r0, s0_send, s0_recv, twin)

    def s0_begin():
        dy_all = dyw[...].reshape(OWN, D)
        for h in range(HPD):
            wp[h, 0:HD, :] = dot_nn(att[h], dy_all).astype(BF16)
        s0_copy.start()

    def s1_copy(o):
        return remote(
            w1.at[lax.rem(y + o, NY)], r1.at[NY - o], s1_send.at[o], s1_recv.at[NY - o], ydev(o)
        )

    def s1_begin():
        s0_copy.wait_recv()
        for h in range(HPD):
            w1[h] = (wp[h, :, near].astype(F32) + r0[h].astype(F32)).astype(BF16)
        for o in order:
            s1_copy(o).start()

    def s2_copy(r):
        return remote(s2.at[r], r2.at[z], s2_send.at[r], s2_recv.at[z], (dp, NX * r + x))

    def s2_begin():
        over_dp = w1[y].astype(F32)
        for o in order:
            remote(w1.at[0], r1.at[o], s1_send.at[o], s1_recv.at[o], ydev(o)).wait_recv()
            over_dp = over_dp + r1[o].astype(F32)
        for r in range(NRED):
            s2[r] = over_dp[:, r * BLK : (r + 1) * BLK].astype(BF16)
        for r in range(NRED):

            @pl.when(r != z)
            def _():
                s2_copy(r).start()

            @pl.when(r == z)
            def _():
                r2[r] = s2[r]

    def s3_copy(t):
        return remote(s3.at[t], h5.at[z], s3_send.at[t], s3_recv.at[z], (dp, owner[t]))

    def s3_begin():
        @pl.when(reducer)
        def _():
            for r in range(NZ):

                @pl.when(r != z)
                def _():
                    remote(s2.at[0], r2.at[r], s2_send.at[0], s2_recv.at[r], (dp, NX * r + x)).wait_recv()

            over_z = r2[0].astype(F32)
            for r in range(1, NZ):
                over_z = over_z + r2[r].astype(F32)
            tot[0:PADW, :] = over_z * (ALL_TOK ** -0.5)
            tot[PADW:, :] = jnp.zeros((8, BLK), F32)
            for t in range(2):
                s3[t] = tot[t * ROWS : t * ROWS + PADR, :].astype(BF16)
            for t in range(2):

                @pl.when(owner[t] != seq)
                def _():
                    s3_copy(t).start()

                @pl.when(owner[t] == seq)
                def _():
                    h5[z] = s3[t]

    def s4_copy(o):
        return remote(h5, h5, s4_send.at[o], s4_recv.at[NY - o], ydev(o))

    def s4_begin():
        @pl.when(collector)
        def _():
            for r in range(NRED):

                @pl.when(jnp.logical_not(is_source(r)))
                def _():
                    remote(s3.at[0], h5.at[r], s3_send.at[0], s3_recv.at[r], (dp, NX * r + src_x)).wait_recv()

            for o in order:
                s4_copy(o).start()

    s5_copy = remote(h5, r3.at[core], s5_send, s5_recv, twin)

    def s5_begin():
        for o in order:

            @pl.when(lax.rem(y + o, NY) == src_y)
            def _():
                remote(h5, h5, s4_send.at[o], s4_recv.at[o], ydev(o)).wait_recv()

        s5_copy.start()
        r3[core] = h5[...]

    def backward(h, i, pair):
        feats = slice(i * HD, (i + 1) * HD)
        for g in range(NG):
            cols = slice(g * QG, (g + 1) * QG)
            q_blk, d_blk, p_all = qt[h, :, cols], dt[h, :, cols], p_scr[g, h]
            delta = jnp.sum(d_blk.astype(F32) * att[h, :, cols].astype(F32), axis=0, keepdims=True)
            for c in range(NCH):
                keys = slice(g * QG + c * BLK, g * QG + (c + 1) * BLK)
                dp_c = dot_nn(vr[h, keys, :], d_blk)
                p = p_scr[g, h, c * BLK : (c + 1) * BLK, :].astype(F32)
                ds_scr[g, c * BLK : (c + 1) * BLK, :] = (SCALE * p * (dp_c - delta)).astype(BF16)
            ds = ds_scr[g]
            dq_acc[pair, feats, cols] = dot_nn(kt[h, :, g * QG : g * QG + KG], ds)
            for acc, left, right in ((dk_acc, q_blk, ds), (dv_acc, d_blk, p_all)):
                add = dot_nt(left, right)
                if g == 0:
                    acc[pair, feats, 0:KG] = add
                else:
                    old = g * QG + KG - QG
                    acc[pair, feats, g * QG : old] += add[:, 0 : KG - QG]
                    acc[pair, feats, old : old + QG] = add[:, KG - QG :]

    def z_copy(t, p, side):
        stage, rz = ((kh_st, rz_k), (vh_st, rz_v))[t]
        zz = down if side == 0 else up
        slots = pl.ds(side * REACH, REACH)
        return remote(
            stage.at[p, slots], rz.at[p, slots], z_send.at[t, p, side], z_recv.at[t, p, side], zdev(zz)
        )

    returns = ((dq_st, rx_q), (t_k, rx_k), (t_v, rx_v))

    def g_copy(t, p, b):
        stage, rx = returns[t]
        return remote(
            stage.at[p, b], rx.at[x, pl.ds(PF * p, PF)], g_send.at[t, p, b], g_recv.at[t, p, x], (dp, NX * z + b)
        )

    def g_start(t, p, b):
        stage, rx = returns[t]

        @pl.when(b != x)
        def _():
            g_copy(t, p, b).start()

        @pl.when(b == x)
        def _():
            rx[b, PF * p : PF * (p + 1), :] = stage[p, b]

    def g_wait(t, p):
        stage, rx = returns[t]
        for b in range(NX):

            @pl.when(b != x)
            def _():
                remote(
                    stage.at[p, b], rx.at[b, pl.ds(PF * p, PF)], g_send.at[t, p, b], g_recv.at[t, p, b],
                    (dp, NX * z + b),
                ).wait_recv()

    def halo_send(p):
        for t, acc, stage in ((0, dk_acc, kh_st), (1, dv_acc, vh_st)):
            for side in range(2):
                for i in range(REACH):
                    slot = i + side * (NX + REACH)
                    stage[p, side * REACH + i] = acc[p, :, slot * BLK : (slot + 1) * BLK].astype(BF16)
                z_copy(t, p, side).start()
        for b in range(NX):
            dq_st[p, b] = dq_acc[p, :, b * BLK : (b + 1) * BLK].astype(BF16)
            g_start(0, p, b)

    def halo_add(p):
        for t, acc, rz in ((0, dk_acc, rz_k), (1, dv_acc, rz_v)):
            for side in range(2):
                z_copy(t, p, side).wait_recv()
            stage = returns[1 + t][0]
            for b in range(NX):
                val = acc[p, :, (REACH + b) * BLK : (REACH + b + 1) * BLK]
                if b >= 1:
                    val = val + rz[p, b - 1].astype(F32)
                if b < REACH:
                    val = val + rz[p, REACH + b].astype(F32)
                stage[p, b] = val.astype(BF16)
                g_start(1 + t, p, b)

    wp[...] = jnp.zeros_like(wp)
    lax.fori_loop(0, HPD, forward, 0)
    for o in (1, 3):
        y_relay_wait(o)
    s0_begin()
    loads[4].wait()
    for b in range(NX):
        d_blk = dot_nt(wbuf[...], dyw[b])
        for h in range(HPD):
            dt[h, :, b * BLK : (b + 1) * BLK] = d_blk[h * HD : (h + 1) * HD].astype(BF16)
    s1_begin()
    backward(0, 0, 0)
    backward(1, 1, 0)
    halo_send(0)
    backward(2, 0, 1)
    s2_begin()
    backward(3, 1, 1)
    halo_send(1)
    s3_begin()
    halo_add(0)
    s4_begin()
    halo_add(1)
    s5_begin()

    for t in range(3):
        for p in range(PAIRS):
            g_wait(t, p)
    for o in order:
        x_copy(0, o, ksend, kwin, REACH).wait_send()
        x_copy(1, o, vsend, vwin, REACH).wait_send()
        x_copy(2, o, qsend, qwin, 0).wait_send()
    for o in (1, 3):
        y_copy(o).wait_send()
        y_relay(o).wait_send()
    for t, win in ((0, kwin), (1, vwin)):
        for xp in range(REACH):
            z_up(t, xp, win).wait_send()
            z_down(t, xp + 1, win).wait_send()
    for t in range(2):
        for p in range(PAIRS):
            for side in range(2):
                z_copy(t, p, side).wait_send()
    for t in range(3):
        for p in range(PAIRS):
            for b in range(NX):

                @pl.when(b != x)
                def _():
                    g_copy(t, p, b).wait_send()

    s0_copy.wait_send()
    for o in order:
        s1_copy(o).wait_send()
    for r in range(NRED):

        @pl.when(r != z)
        def _():
            s2_copy(r).wait_send()

    @pl.when(reducer)
    def _():
        for t in range(2):

            @pl.when(owner[t] != seq)
            def _():
                s3_copy(t).wait_send()

    @pl.when(collector)
    def _():
        for o in order:
            s4_copy(o).wait_send()

    remote(h5, r3.at[1 - core], s5_send, s5_recv, twin).wait()


def main_call(lengths, queries, keys, values, out_grad, out_weight):
    dma = pltpu.SemaphoreType.DMA
    b16 = lambda *shape: pltpu.VMEM(shape, BF16)
    f32 = lambda *shape: pltpu.VMEM(shape, F32)
    back = jax.ShapeDtypeStruct((NX, FEAT, BLK), BF16)
    return pl.pallas_call(
        main_kernel,
        out_shape=(back, back, back, jax.ShapeDtypeStruct((NCORE, NRED, PADR, BLK), BF16)),
        in_specs=[pl.BlockSpec(memory_space=pltpu.SMEM)] + [HB] * 5,
        out_specs=(VM,) * 4,
        scratch_shapes=[
            b16(BLK, D), b16(BLK, D), b16(BLK, D), b16(FEAT, D), b16(NX, BLK, D),
            b16(D, BLK), b16(D, BLK), b16(D, BLK),
            b16(SLOTS, FEAT, BLK), b16(SLOTS, FEAT, BLK), b16(NX, FEAT, BLK),
            b16(HPD, HD, OWN), b16(HPD, HD, WIDE), b16(HPD, HD, WIDE), b16(HPD, WIDE, HD), b16(HPD, WIDE, HD),
            b16(HPD, HD, OWN),
            f32(NG, KG, QG), b16(NG, HPD, KG, QG), b16(NG, KG, QG), b16(HPD, HD, OWN),
            f32(PAIRS, PF, OWN), f32(PAIRS, PF, WIDE), f32(PAIRS, PF, WIDE),
            b16(PAIRS, NX, PF, BLK), b16(PAIRS, 2 * REACH, PF, BLK), b16(PAIRS, 2 * REACH, PF, BLK),
            b16(PAIRS, 2 * REACH, PF, BLK), b16(PAIRS, 2 * REACH, PF, BLK),
            b16(PAIRS, NX, PF, BLK), b16(PAIRS, NX, PF, BLK),
            b16(HPD, PADW, D), b16(HPD, PADW, CHUNK), b16(HPD, PADW, CHUNK), b16(NY, PADW, CHUNK),
            b16(NRED, PADW, BLK), b16(NZ, PADW, BLK), f32(PADW + 8, BLK), b16(2, PADR, BLK), b16(NRED, PADR, BLK),
            dma((5,)), dma((3, NX)), dma((3, NX)), dma((4,)), dma((4,)), dma((2, 2, NX)), dma((2, 2, NX)),
            dma((2, PAIRS, 2)), dma((2, PAIRS, 2)), dma((3, PAIRS, NX)), dma((3, PAIRS, NX)),
            dma, dma, dma((NY,)), dma((NY,)), dma((NRED,)), dma((NZ,)), dma((2,)), dma((NRED,)),
            dma((NY,)), dma((NY,)), dma, dma,
        ],
        compiler_params=pltpu.CompilerParams(
            collective_id=0, has_side_effects=True, vmem_limit_bytes=60 * 2**20
        ),
        name="attention_backward",
    )(lengths, queries, keys, values, out_grad, out_weight)


def finish_kernel(rq, rk, rv, rw, gq, gk, gv, gw, inb, outb, wbuf, i_sem, o_sem):
    gets = [pltpu.make_async_copy(r, inb.at[t], i_sem.at[t]) for t, r in enumerate((rq, rk, rv))]
    puts = [pltpu.make_async_copy(outb.at[t], g.at[0], o_sem.at[t]) for t, g in enumerate((gq, gk, gv))]
    for copy in gets:
        copy.start()
    for t in range(3):
        gets[t].wait()
        for i in range(D // BLK):
            outb[t, :, i * BLK : (i + 1) * BLK] = inb[t, i * BLK : (i + 1) * BLK, :].astype(F32).T
        puts[t].start()
    for c in range(NCORE):
        for r in range(NRED):
            col = c * CSTEP + r * BLK
            wbuf[:, col : col + BLK] = rw[c, r, 0:ROWS, :].astype(F32)
    last = pltpu.make_async_copy(wbuf, gw, o_sem.at[3])
    last.start()
    for copy in puts:
        copy.wait()
    last.wait()


def finish(rq, rk, rv, rw):
    grad = jax.ShapeDtypeStruct((1, BLK, D), F32)
    return pl.pallas_call(
        finish_kernel,
        out_shape=(grad, grad, grad, jax.ShapeDtypeStruct((ROWS, D), F32)),
        in_specs=[HB] * 3 + [VM],
        out_specs=(HB,) * 4,
        scratch_shapes=[
            pltpu.VMEM((3, D, BLK), BF16), pltpu.VMEM((3, BLK, D), F32), pltpu.VMEM((ROWS, D), F32),
            pltpu.SemaphoreType.DMA((3,)), pltpu.SemaphoreType.DMA((4,)),
        ],
        name="outputs",
    )(*[r.reshape(D, BLK) for r in (rq, rk, rv)], rw)


def body(queries, keys, values, out_weight, out_grad, lengths):
    return finish(*main_call(lengths, queries, keys, values, out_grad, out_weight))


def solution(mesh):
    rows = P("dp", "seq", None)
    return jax.shard_map(
        body,
        mesh=mesh,
        in_specs=(rows, rows, rows, P(), rows, P("dp", None)),
        out_specs=(rows, rows, rows, P("seq", None)),
        check_vma=False,
    )
```

```python
import math

import jax
import jax.numpy as jnp
from jax import lax
from jax.experimental import pallas as pl
from jax.experimental.pallas import tpu as pltpu
from jax.sharding import PartitionSpec as P

NX, NZ = 4, 8
NY, NCORE = 4, 2
NDP = NY * NCORE
BLK = 128
HEADS, HD = 16, 72
HPD = HEADS // NX
FEAT = HPD * HD
D = HEADS * HD
REACH = 3
SLOTS = NX + 2 * REACH
WIDE = SLOTS * BLK
OWN = NX * BLK
NIMG = 20
TOKENS = 4096
ALL_TOK = 32768
SCALE = HD ** -0.5
LOG2E = math.log2(math.e)
NEG = -1e30
QG = 256
NG = OWN // QG
KG = QG + 2 * REACH * BLK
NCH = KG // BLK
PAIRS = HPD // 2
PART = 3 * BLK
PF = 2 * HD
PADW = 80
CHUNK = 640
CSTEP = 512
NRED = 5
ROWS = D // (NX * NZ)
PADR = 48

F32, BF16 = jnp.float32, jnp.bfloat16
MESH = pl.DeviceIdType.MESH
VM = pl.BlockSpec(memory_space=pltpu.VMEM)
HB = pl.BlockSpec(memory_space=pltpu.HBM)


def remote(src, dst, send, recv, device):
    return pltpu.make_async_remote_copy(
        src_ref=src, dst_ref=dst, send_sem=send, recv_sem=recv, device_id=device, device_id_type=MESH
    )


def hello(barrier, device):
    pl.semaphore_signal(barrier, inc=1, device_id=device, device_id_type=MESH)


def dot_nn(a, b):
    return lax.dot_general(a, b, (((1,), (0,)), ((), ())), preferred_element_type=F32)


def dot_nt(a, b):
    return lax.dot_general(a, b, (((1,), (1,)), ((), ())), preferred_element_type=F32)


def main_kernel(
    len_ref, q_hbm, k_hbm, v_hbm, dy_hbm, w_hbm,
    rx_q, rx_k, rx_v, r3,
    kin, vin, qin, wbuf, dyw, ksend, vsend, qsend, kwin, vwin, qwin,
    qt, kt, vt, kr, vr, dt, s_scr, p_scr, ds_scr, att, dq_acc, dk_acc, dv_acc,
    dq_st, kh_st, vh_st, rz_k, rz_v, t_k, t_v,
    wp, r0, w1, r1, s2, r2, tot, s3, h5,
    l_sem, x_send, x_recv, y_send, y_recv, f_send, f_recv, z_send, z_recv, g_send, g_recv,
    s0_send, s0_recv, s1_send, s1_recv, s2_send, s2_recv, s3_send, s3_recv, s4_send, s4_recv, s5_send, s5_recv,
):
    dp, seq = lax.axis_index("dp"), lax.axis_index("seq")
    z, x = lax.div(seq, NX), lax.rem(seq, NX)
    y, core = lax.div(dp, NCORE), lax.rem(dp, NCORE)
    up, down = lax.rem(z + 1, NZ), lax.rem(z + NZ - 1, NZ)
    barrier = pltpu.get_barrier_semaphore()
    reducer = z < NRED
    order = (1, 3, 2)

    def xdev(o):
        return (dp, NX * z + lax.rem(x + o, NX))

    def zdev(zz):
        return (dp, NX * zz + x)

    def ydev(o):
        return (NCORE * lax.rem(y + o, NY) + core, seq)

    twin = (dp + 1 - 2 * core, seq)

    loads = [
        pltpu.make_async_copy(k_hbm.at[0], kin, l_sem.at[0]),
        pltpu.make_async_copy(v_hbm.at[0], vin, l_sem.at[1]),
        pltpu.make_async_copy(q_hbm.at[0], qin, l_sem.at[2]),
        pltpu.make_async_copy(dy_hbm.at[0], dyw.at[x], l_sem.at[3]),
        pltpu.make_async_copy(w_hbm.at[pl.ds(pl.multiple_of(FEAT * x, 32), FEAT)], wbuf, l_sem.at[4]),
    ]
    for copy in loads:
        copy.start()

    head = HPD * x + y
    owner = [2 * head, 2 * head + 1]
    my_head = lax.div(seq, 2)
    src_x, src_y = lax.div(my_head, HPD), lax.rem(my_head, HPD)
    collector = src_y == y

    def is_source(r):
        return jnp.logical_and(src_x == x, z == r)

    for o in order:
        hello(barrier, xdev(o))
    for zz in (up, down):
        hello(barrier, zdev(zz))
    hello(barrier, twin)
    for o in order:
        hello(barrier, ydev(o))

    @pl.when(reducer)
    def _():
        for o in range(1, NZ):
            hello(barrier, zdev(lax.rem(z + o, NZ)))

    for r in range(NRED):

        @pl.when(jnp.logical_and(collector, jnp.logical_not(is_source(r))))
        def _():
            hello(barrier, (dp, NX * r + src_x))

    to_reducers = jnp.where(reducer, NRED - 1, NRED)
    mine_too = jnp.int32(0)
    for t in range(2):
        mine_too = mine_too + jnp.where(owner[t] == seq, 1, 0)
    to_owners = jnp.where(reducer, 2 - mine_too, 0)

    def turn(src, dst):
        for i in range(D // BLK):
            tile = src[:, i * BLK : (i + 1) * BLK].astype(F32)
            dst[i * BLK : (i + 1) * BLK, :] = tile.T.astype(BF16)

    def part(ref, xp):
        return ref.at[pl.ds(pl.multiple_of(FEAT * xp, 32), FEAT)]

    def x_copy(t, o, src, win, base):
        xp = lax.rem(x + o, NX)
        return remote(part(src, xp), win.at[base + x], x_send.at[t, o], x_recv.at[t, NX - o], xdev(o))

    def x_wait(t, o, src, win, base):
        xp = lax.rem(x + o, NX)
        remote(part(src, xp), win.at[base + xp], x_send.at[t, o], x_recv.at[t, o], xdev(o)).wait_recv()

    def y_rows(o, part):
        return pl.ds((o // 2 if part == 0 else 1 - o // 2) * (BLK // 2), BLK // 2)

    def y_copy(o, part):
        block = dyw.at[x, y_rows(NX - o, part)]
        there = (NX - o) // 2 * 2 + part
        return remote(block, block, y_send.at[o // 2 * 2 + part], y_recv.at[there], xdev(o))

    def y_wait(o, part):
        block = dyw.at[lax.rem(x + o, NX), y_rows(o, part)]
        here = o // 2 * 2 + part
        remote(block, block, y_send.at[here], y_recv.at[here], xdev(o)).wait_recv()

    def y_relay(o):
        block = dyw.at[lax.rem(x + o, NX), y_rows(o, 0)]
        return remote(block, block, y_send.at[4 + o // 2], y_recv.at[4 + o // 2], xdev(NX - o))

    def y_relay_wait(o):
        block = dyw.at[lax.rem(x + 2, NX), y_rows(o, 0)]
        remote(block, block, y_send.at[4 + o // 2], y_recv.at[4 + o // 2], xdev(NX - o)).wait_recv()

    mine = pl.ds(pl.multiple_of(FEAT * x, 32), FEAT)
    loads[0].wait()
    turn(kin, ksend)
    pl.semaphore_wait(barrier, 2 * (NX - 1) + 3 + to_reducers + to_owners)
    for o in order:
        x_copy(0, o, ksend, kwin, REACH).start()
    loads[1].wait()
    turn(vin, vsend)
    for o in order:
        x_copy(1, o, vsend, vwin, REACH).start()
    loads[2].wait()
    turn(qin, qsend)
    for o in order:
        x_copy(2, o, qsend, qwin, 0).start()
    loads[3].wait()
    for n in range(2):
        for o in (1, 3):
            y_copy(o, n).start()
    kwin[REACH + x] = ksend[mine, :]
    vwin[REACH + x] = vsend[mine, :]
    qwin[x] = qsend[mine, :]

    def z_up(t, xp, win):
        return remote(
            win.at[REACH + xp], win.at[xp + NX + REACH], f_send.at[t, 0, xp], f_recv.at[t, 0, xp], zdev(down)
        )

    def z_down(t, xp, win):
        return remote(win.at[REACH + xp], win.at[xp - 1], f_send.at[t, 1, xp], f_recv.at[t, 1, xp], zdev(up))

    for t, src, win in ((0, ksend, kwin), (1, vsend, vwin)):
        for o in (0,) + order:
            xp = lax.rem(x + o, NX)
            if o:
                x_wait(t, o, src, win, REACH)

            @pl.when(xp < REACH)
            def _():
                z_up(t, xp, win).start()

            @pl.when(xp >= 1)
            def _():
                z_down(t, xp, win).start()

    def unpack(win, slot, t_out, r_out):
        val = win[slot].astype(F32)
        cols = pl.ds(pl.multiple_of(slot * BLK, BLK), BLK)
        for h in range(HPD):
            piece = val[h * HD : (h + 1) * HD]
            t_out[h, :, cols] = piece.astype(BF16)
            if r_out is not None:
                r_out[h, cols, :] = piece.T.astype(BF16)

    def unpack_kv(slot, carry):
        unpack(kwin, slot, kt, kr)
        unpack(vwin, slot, vt, vr)
        return carry

    def unpack_q(slot, carry):
        unpack(qwin, slot, qt, None)
        return carry

    lax.fori_loop(REACH, REACH + NX, unpack_kv, 0)
    for o in order:
        x_wait(2, o, qsend, qwin, 0)
    lax.fori_loop(0, NX, unpack_q, 0)
    for t, win in ((0, kwin), (1, vwin)):
        for xp in range(REACH):
            z_up(t, xp, win).wait_recv()
            z_down(t, xp + 1, win).wait_recv()
    lax.fori_loop(0, REACH, unpack_kv, 0)
    lax.fori_loop(REACH + NX, SLOTS, unpack_kv, 0)
    for o in (1, 3):
        y_wait(o, 0)
        y_relay(o).start()

    first = (NX * z - REACH) * BLK
    rows = lax.broadcasted_iota(jnp.int32, (BLK, QG), 0)
    ends = []
    total = jnp.int32(0)
    for i in range(NIMG):
        total = total + len_ref[0, i]
        ends.append(total)

    spans = []
    for g in range(NG):
        pos = NX * z * BLK + g * QG + lax.broadcasted_iota(jnp.int32, (8, QG), 1)
        lo = jnp.zeros_like(pos)
        hi = jnp.full_like(pos, TOKENS)
        for e in ends:
            lo = jnp.where(e <= pos, e, lo)
        for e in ends[::-1]:
            hi = jnp.where(e > pos, e, hi)
        spans.append((lo[0:1] - first - g * QG, hi[0:1] - first - g * QG))

    def forward(h, carry):
        for g in range(NG):
            lo, hi = spans[g]
            q_blk = qt[h, :, g * QG : (g + 1) * QG]
            top = jnp.full((1, QG), NEG, F32)
            for c in range(NCH):
                keys = slice(g * QG + c * BLK, g * QG + (c + 1) * BLK)
                s = dot_nn(kr[h, keys, :], q_blk)
                keep = jnp.logical_and(rows >= lo - c * BLK, rows < hi - c * BLK)
                s = jnp.where(keep, s, NEG)
                s_scr[g, c * BLK : (c + 1) * BLK, :] = s
                top = jnp.maximum(top, jnp.max(s, axis=0, keepdims=True))
            norm = jnp.zeros((1, QG), F32)
            for c in range(NCH):
                e = jnp.exp2((s_scr[g, c * BLK : (c + 1) * BLK, :] - top) * (SCALE * LOG2E))
                s_scr[g, c * BLK : (c + 1) * BLK, :] = e
                norm = norm + jnp.sum(e, axis=0, keepdims=True)
            inv = 1.0 / norm
            for c in range(NCH):
                p_scr[g, h, c * BLK : (c + 1) * BLK, :] = (
                    s_scr[g, c * BLK : (c + 1) * BLK, :] * inv
                ).astype(BF16)
            mixed = dot_nn(vt[h, :, g * QG : g * QG + KG], p_scr[g, h])
            att[pl.ds(pl.multiple_of(h * HD, 8), HD), g * QG : (g + 1) * QG] = mixed
        return carry

    far = pl.ds(pl.multiple_of(CSTEP * (1 - core), BLK), CHUNK)
    near = pl.ds(pl.multiple_of(CSTEP * core, BLK), CHUNK)
    s0_copy = remote(wp.at[:, :, far], r0, s0_send, s0_recv, twin)

    def s0_begin():
        attended = att[...].astype(BF16)
        for i in range(D // PART):
            cols = slice(i * PART, (i + 1) * PART)
            share = dot_nn(attended, dyw[:, :, cols].reshape(OWN, PART))
            for h in range(HPD):
                wp[h, 0:HD, cols] = share[h * HD : (h + 1) * HD].astype(BF16)
        s0_copy.start()

    def s1_copy(o):
        return remote(
            w1.at[lax.rem(y + o, NY)], r1.at[NY - o], s1_send.at[o], s1_recv.at[NY - o], ydev(o)
        )

    def s1_begin():
        s0_copy.wait_recv()
        for h in range(HPD):
            w1[h] = (wp[h, :, near].astype(F32) + r0[h].astype(F32)).astype(BF16)
        for o in order:
            s1_copy(o).start()

    def s2_copy(r):
        return remote(s2.at[r], r2.at[z], s2_send.at[r], s2_recv.at[z], (dp, NX * r + x))

    def s2_begin():
        over_dp = w1[y].astype(F32)
        for o in order:
            remote(w1.at[0], r1.at[o], s1_send.at[o], s1_recv.at[o], ydev(o)).wait_recv()
            over_dp = over_dp + r1[o].astype(F32)
        for r in range(NRED):
            s2[r] = over_dp[:, r * BLK : (r + 1) * BLK].astype(BF16)
        for r in range(NRED):

            @pl.when(r != z)
            def _():
                s2_copy(r).start()

            @pl.when(r == z)
            def _():
                r2[r] = s2[r]

    def s3_copy(t):
        return remote(s3.at[t], h5.at[z], s3_send.at[t], s3_recv.at[z], (dp, owner[t]))

    def s3_begin():
        @pl.when(reducer)
        def _():
            for r in range(NZ):

                @pl.when(r != z)
                def _():
                    remote(s2.at[0], r2.at[r], s2_send.at[0], s2_recv.at[r], (dp, NX * r + x)).wait_recv()

            over_z = r2[0].astype(F32)
            for r in range(1, NZ):
                over_z = over_z + r2[r].astype(F32)
            tot[0:PADW, :] = over_z * (ALL_TOK ** -0.5)
            tot[PADW:, :] = jnp.zeros((8, BLK), F32)
            for t in range(2):
                s3[t] = tot[t * ROWS : t * ROWS + PADR, :].astype(BF16)
            for t in range(2):

                @pl.when(owner[t] != seq)
                def _():
                    s3_copy(t).start()

                @pl.when(owner[t] == seq)
                def _():
                    h5[z] = s3[t]

    def s4_copy(o):
        return remote(h5, h5, s4_send.at[o], s4_recv.at[NY - o], ydev(o))

    def s4_begin():
        @pl.when(collector)
        def _():
            for r in range(NRED):

                @pl.when(jnp.logical_not(is_source(r)))
                def _():
                    remote(s3.at[0], h5.at[r], s3_send.at[0], s3_recv.at[r], (dp, NX * r + src_x)).wait_recv()

            for o in order:
                s4_copy(o).start()

    s5_copy = remote(h5, r3.at[core], s5_send, s5_recv, twin)

    def s5_begin():
        for o in order:

            @pl.when(lax.rem(y + o, NY) == src_y)
            def _():
                remote(h5, h5, s4_send.at[o], s4_recv.at[o], ydev(o)).wait_recv()

        s5_copy.start()
        r3[core] = h5[...]

    def backward(h, i, pair):
        feats = slice(i * HD, (i + 1) * HD)
        for g in range(NG):
            cols = slice(g * QG, (g + 1) * QG)
            q_blk, d_blk, p_all = qt[h, :, cols], dt[h, :, cols], p_scr[g, h]
            mixed = att[h * HD : (h + 1) * HD, cols].astype(BF16).astype(F32)
            delta = jnp.sum(d_blk.astype(F32) * mixed, axis=0, keepdims=True)
            for c in range(NCH):
                keys = slice(g * QG + c * BLK, g * QG + (c + 1) * BLK)
                dp_c = dot_nn(vr[h, keys, :], d_blk)
                p = p_scr[g, h, c * BLK : (c + 1) * BLK, :].astype(F32)
                ds_scr[g, c * BLK : (c + 1) * BLK, :] = (SCALE * p * (dp_c - delta)).astype(BF16)
            ds = ds_scr[g]
            dq_acc[pair, feats, cols] = dot_nn(kt[h, :, g * QG : g * QG + KG], ds)
            for acc, left, right in ((dk_acc, q_blk, ds), (dv_acc, d_blk, p_all)):
                add = dot_nt(left, right)
                if g == 0:
                    acc[pair, feats, 0:KG] = add
                else:
                    old = g * QG + KG - QG
                    acc[pair, feats, g * QG : old] += add[:, 0 : KG - QG]
                    acc[pair, feats, old : old + QG] = add[:, KG - QG :]

    def z_copy(t, p, side):
        stage, rz = ((kh_st, rz_k), (vh_st, rz_v))[t]
        zz = down if side == 0 else up
        slots = pl.ds(side * REACH, REACH)
        return remote(
            stage.at[p, slots], rz.at[p, slots], z_send.at[t, p, side], z_recv.at[t, p, side], zdev(zz)
        )

    returns = ((dq_st, rx_q), (t_k, rx_k), (t_v, rx_v))

    def g_copy(t, p, b):
        stage, rx = returns[t]
        return remote(
            stage.at[p, b], rx.at[x, pl.ds(PF * p, PF)], g_send.at[t, p, b], g_recv.at[t, p, x], (dp, NX * z + b)
        )

    def g_start(t, p, b):
        stage, rx = returns[t]

        @pl.when(b != x)
        def _():
            g_copy(t, p, b).start()

        @pl.when(b == x)
        def _():
            rx[b, PF * p : PF * (p + 1), :] = stage[p, b]

    def g_wait(t, p):
        stage, rx = returns[t]
        for b in range(NX):

            @pl.when(b != x)
            def _():
                remote(
                    stage.at[p, b], rx.at[b, pl.ds(PF * p, PF)], g_send.at[t, p, b], g_recv.at[t, p, b],
                    (dp, NX * z + b),
                ).wait_recv()

    def halo_send(p):
        for t, acc, stage in ((0, dk_acc, kh_st), (1, dv_acc, vh_st)):
            for side in range(2):
                for i in range(REACH):
                    slot = i + side * (NX + REACH)
                    stage[p, side * REACH + i] = acc[p, :, slot * BLK : (slot + 1) * BLK].astype(BF16)
                z_copy(t, p, side).start()
        for b in range(NX):
            dq_st[p, b] = dq_acc[p, :, b * BLK : (b + 1) * BLK].astype(BF16)
            g_start(0, p, b)

    def halo_add(p):
        for t, acc, rz in ((0, dk_acc, rz_k), (1, dv_acc, rz_v)):
            for side in range(2):
                z_copy(t, p, side).wait_recv()
            stage = returns[1 + t][0]
            for b in range(NX):
                val = acc[p, :, (REACH + b) * BLK : (REACH + b + 1) * BLK]
                if b >= 1:
                    val = val + rz[p, b - 1].astype(F32)
                if b < REACH:
                    val = val + rz[p, REACH + b].astype(F32)
                stage[p, b] = val.astype(BF16)
                g_start(1 + t, p, b)

    wp[...] = jnp.zeros_like(wp)
    lax.fori_loop(0, HPD, forward, 0)
    for o in (1, 3):
        y_wait(o, 1)
    for o in (1, 3):
        y_relay_wait(o)
    s0_begin()
    loads[4].wait()
    for g in range(NG):
        d_blk = dot_nt(wbuf[...], dyw[g * 2 : g * 2 + 2].reshape(QG, D))
        for h in range(HPD):
            dt[h, :, g * QG : (g + 1) * QG] = d_blk[h * HD : (h + 1) * HD].astype(BF16)
    s1_begin()
    backward(0, 0, 0)
    backward(1, 1, 0)
    halo_send(0)
    backward(2, 0, 1)
    backward(3, 1, 1)
    s2_begin()
    halo_send(1)
    halo_add(0)
    s3_begin()
    s4_begin()
    halo_add(1)
    s5_begin()

    for t in range(3):
        for p in range(PAIRS):
            g_wait(t, p)
    for o in order:
        x_copy(0, o, ksend, kwin, REACH).wait_send()
        x_copy(1, o, vsend, vwin, REACH).wait_send()
        x_copy(2, o, qsend, qwin, 0).wait_send()
    for o in (1, 3):
        y_copy(o, 0).wait_send()
        y_copy(o, 1).wait_send()
        y_relay(o).wait_send()
    for t, win in ((0, kwin), (1, vwin)):
        for xp in range(REACH):
            z_up(t, xp, win).wait_send()
            z_down(t, xp + 1, win).wait_send()
    for t in range(2):
        for p in range(PAIRS):
            for side in range(2):
                z_copy(t, p, side).wait_send()
    for t in range(3):
        for p in range(PAIRS):
            for b in range(NX):

                @pl.when(b != x)
                def _():
                    g_copy(t, p, b).wait_send()

    s0_copy.wait_send()
    for o in order:
        s1_copy(o).wait_send()
    for r in range(NRED):

        @pl.when(r != z)
        def _():
            s2_copy(r).wait_send()

    @pl.when(reducer)
    def _():
        for t in range(2):

            @pl.when(owner[t] != seq)
            def _():
                s3_copy(t).wait_send()

    @pl.when(collector)
    def _():
        for o in order:
            s4_copy(o).wait_send()

    remote(h5, r3.at[1 - core], s5_send, s5_recv, twin).wait()


def main_call(lengths, queries, keys, values, out_grad, out_weight):
    dma = pltpu.SemaphoreType.DMA
    b16 = lambda *shape: pltpu.VMEM(shape, BF16)
    f32 = lambda *shape: pltpu.VMEM(shape, F32)
    back = jax.ShapeDtypeStruct((NX, FEAT, BLK), BF16)
    return pl.pallas_call(
        main_kernel,
        out_shape=(back, back, back, jax.ShapeDtypeStruct((NCORE, NRED, PADR, BLK), BF16)),
        in_specs=[pl.BlockSpec(memory_space=pltpu.SMEM)] + [HB] * 5,
        out_specs=(VM,) * 4,
        scratch_shapes=[
            b16(BLK, D), b16(BLK, D), b16(BLK, D), b16(FEAT, D), b16(NX, BLK, D),
            b16(D, BLK), b16(D, BLK), b16(D, BLK),
            b16(SLOTS, FEAT, BLK), b16(SLOTS, FEAT, BLK), b16(NX, FEAT, BLK),
            b16(HPD, HD, OWN), b16(HPD, HD, WIDE), b16(HPD, HD, WIDE), b16(HPD, WIDE, HD), b16(HPD, WIDE, HD),
            b16(HPD, HD, OWN),
            f32(NG, KG, QG), b16(NG, HPD, KG, QG), b16(NG, KG, QG), f32(FEAT, OWN),
            f32(PAIRS, PF, OWN), f32(PAIRS, PF, WIDE), f32(PAIRS, PF, WIDE),
            b16(PAIRS, NX, PF, BLK), b16(PAIRS, 2 * REACH, PF, BLK), b16(PAIRS, 2 * REACH, PF, BLK),
            b16(PAIRS, 2 * REACH, PF, BLK), b16(PAIRS, 2 * REACH, PF, BLK),
            b16(PAIRS, NX, PF, BLK), b16(PAIRS, NX, PF, BLK),
            b16(HPD, PADW, D), b16(HPD, PADW, CHUNK), b16(HPD, PADW, CHUNK), b16(NY, PADW, CHUNK),
            b16(NRED, PADW, BLK), b16(NZ, PADW, BLK), f32(PADW + 8, BLK), b16(2, PADR, BLK), b16(NRED, PADR, BLK),
            dma((5,)), dma((3, NX)), dma((3, NX)), dma((6,)), dma((6,)), dma((2, 2, NX)), dma((2, 2, NX)),
            dma((2, PAIRS, 2)), dma((2, PAIRS, 2)), dma((3, PAIRS, NX)), dma((3, PAIRS, NX)),
            dma, dma, dma((NY,)), dma((NY,)), dma((NRED,)), dma((NZ,)), dma((2,)), dma((NRED,)),
            dma((NY,)), dma((NY,)), dma, dma,
        ],
        compiler_params=pltpu.CompilerParams(
            collective_id=0, has_side_effects=True, vmem_limit_bytes=60 * 2**20
        ),
        name="attention_backward",
    )(lengths, queries, keys, values, out_grad, out_weight)


def finish_kernel(rq, rk, rv, rw, gq, gk, gv, gw, inb, outb, wbuf, i_sem, o_sem):
    gets = [pltpu.make_async_copy(r, inb.at[t], i_sem.at[t]) for t, r in enumerate((rq, rk, rv))]
    puts = [pltpu.make_async_copy(outb.at[t], g.at[0], o_sem.at[t]) for t, g in enumerate((gq, gk, gv))]
    for copy in gets:
        copy.start()
    for t in range(3):
        gets[t].wait()
        for i in range(D // BLK):
            outb[t, :, i * BLK : (i + 1) * BLK] = inb[t, i * BLK : (i + 1) * BLK, :].astype(F32).T
        puts[t].start()
    for c in range(NCORE):
        for r in range(NRED):
            col = c * CSTEP + r * BLK
            wbuf[:, col : col + BLK] = rw[c, r, 0:ROWS, :].astype(F32)
    last = pltpu.make_async_copy(wbuf, gw, o_sem.at[3])
    last.start()
    for copy in puts:
        copy.wait()
    last.wait()


def finish(rq, rk, rv, rw):
    grad = jax.ShapeDtypeStruct((1, BLK, D), F32)
    return pl.pallas_call(
        finish_kernel,
        out_shape=(grad, grad, grad, jax.ShapeDtypeStruct((ROWS, D), F32)),
        in_specs=[HB] * 3 + [VM],
        out_specs=(HB,) * 4,
        scratch_shapes=[
            pltpu.VMEM((3, D, BLK), BF16), pltpu.VMEM((3, BLK, D), F32), pltpu.VMEM((ROWS, D), F32),
            pltpu.SemaphoreType.DMA((3,)), pltpu.SemaphoreType.DMA((4,)),
        ],
        name="outputs",
    )(*[r.reshape(D, BLK) for r in (rq, rk, rv)], rw)


def body(queries, keys, values, out_weight, out_grad, lengths):
    return finish(*main_call(lengths, queries, keys, values, out_grad, out_weight))


def solution(mesh):
    rows = P("dp", "seq", None)
    return jax.shard_map(
        body,
        mesh=mesh,
        in_specs=(rows, rows, rows, P(), rows, P("dp", None)),
        out_specs=(rows, rows, rows, P("seq", None)),
        check_vma=False,
    )
```

```python
import math

import jax
import jax.numpy as jnp
from jax import lax
from jax.experimental import pallas as pl
from jax.experimental.pallas import tpu as pltpu
from jax.sharding import PartitionSpec as P

NX, NZ = 4, 8
NY, NCORE = 4, 2
NDP = NY * NCORE
BLK = 128
HEADS, HD = 16, 72
HPD = HEADS // NX
FEAT = HPD * HD
D = HEADS * HD
REACH = 3
SLOTS = NX + 2 * REACH
WIDE = SLOTS * BLK
OWN = NX * BLK
NIMG = 20
TOKENS = 4096
ALL_TOK = 32768
SCALE = HD ** -0.5
LOG2E = math.log2(math.e)
NEG = -1e30
QG = 256
NG = OWN // QG
KG = QG + 2 * REACH * BLK
NCH = KG // BLK
PAIRS = HPD // 2
PART = 3 * BLK
PF = 2 * HD
PADW = 80
CHUNK = 640
CSTEP = 512
NRED = 5
ROWS = D // (NX * NZ)
PADR = 48

F32, BF16 = jnp.float32, jnp.bfloat16
MESH = pl.DeviceIdType.MESH
VM = pl.BlockSpec(memory_space=pltpu.VMEM)
HB = pl.BlockSpec(memory_space=pltpu.HBM)


def remote(src, dst, send, recv, device):
    return pltpu.make_async_remote_copy(
        src_ref=src, dst_ref=dst, send_sem=send, recv_sem=recv, device_id=device, device_id_type=MESH
    )


def hello(barrier, device):
    pl.semaphore_signal(barrier, inc=1, device_id=device, device_id_type=MESH)


def dot_nn(a, b):
    return lax.dot_general(a, b, (((1,), (0,)), ((), ())), preferred_element_type=F32)


def dot_nt(a, b):
    return lax.dot_general(a, b, (((1,), (1,)), ((), ())), preferred_element_type=F32)


def main_kernel(
    len_ref, q_hbm, k_hbm, v_hbm, dy_hbm, w_hbm,
    rx_q, rx_k, rx_v, r3,
    kin, vin, qin, wbuf, dyw, ksend, vsend, qsend, kwin, vwin, qwin,
    qt, kt, vt, kr, vr, dt, s_scr, p_scr, ds_scr, att, dq_acc, dk_acc, dv_acc,
    dq_st, kh_st, vh_st, rz_k, rz_v, t_k, t_v,
    wp, r0, w1, r1, s2, r2, tot, s3, h5,
    l_sem, x_send, x_recv, y_send, y_recv, f_send, f_recv, z_send, z_recv, g_send, g_recv,
    s0_send, s0_recv, s1_send, s1_recv, s2_send, s2_recv, s3_send, s3_recv, s4_send, s4_recv, s5_send, s5_recv,
):
    dp, seq = lax.axis_index("dp"), lax.axis_index("seq")
    z, x = lax.div(seq, NX), lax.rem(seq, NX)
    y, core = lax.div(dp, NCORE), lax.rem(dp, NCORE)
    up, down = lax.rem(z + 1, NZ), lax.rem(z + NZ - 1, NZ)
    barrier = pltpu.get_barrier_semaphore()
    reducer = z < NRED
    order = (1, 3, 2)

    def xdev(o):
        return (dp, NX * z + lax.rem(x + o, NX))

    def zdev(zz):
        return (dp, NX * zz + x)

    def ydev(o):
        return (NCORE * lax.rem(y + o, NY) + core, seq)

    twin = (dp + 1 - 2 * core, seq)

    loads = [
        pltpu.make_async_copy(k_hbm.at[0], kin, l_sem.at[0]),
        pltpu.make_async_copy(v_hbm.at[0], vin, l_sem.at[1]),
        pltpu.make_async_copy(q_hbm.at[0], qin, l_sem.at[2]),
        pltpu.make_async_copy(dy_hbm.at[0], dyw.at[x], l_sem.at[3]),
        pltpu.make_async_copy(w_hbm.at[pl.ds(pl.multiple_of(FEAT * x, 32), FEAT)], wbuf, l_sem.at[4]),
    ]
    for copy in loads:
        copy.start()

    head = HPD * x + y
    owner = [2 * head, 2 * head + 1]
    my_head = lax.div(seq, 2)
    src_x, src_y = lax.div(my_head, HPD), lax.rem(my_head, HPD)
    collector = src_y == y

    def is_source(r):
        return jnp.logical_and(src_x == x, z == r)

    for o in order:
        hello(barrier, xdev(o))
    for zz in (up, down):
        hello(barrier, zdev(zz))
    hello(barrier, twin)
    for o in order:
        hello(barrier, ydev(o))

    @pl.when(reducer)
    def _():
        for o in range(1, NZ):
            hello(barrier, zdev(lax.rem(z + o, NZ)))

    for r in range(NRED):

        @pl.when(jnp.logical_and(collector, jnp.logical_not(is_source(r))))
        def _():
            hello(barrier, (dp, NX * r + src_x))

    to_reducers = jnp.where(reducer, NRED - 1, NRED)
    mine_too = jnp.int32(0)
    for t in range(2):
        mine_too = mine_too + jnp.where(owner[t] == seq, 1, 0)
    to_owners = jnp.where(reducer, 2 - mine_too, 0)

    def turn(src, dst):
        for i in range(D // BLK):
            tile = src[:, i * BLK : (i + 1) * BLK].astype(F32)
            dst[i * BLK : (i + 1) * BLK, :] = tile.T.astype(BF16)

    def part(ref, xp):
        return ref.at[pl.ds(pl.multiple_of(FEAT * xp, 32), FEAT)]

    def x_copy(t, o, src, win, base):
        xp = lax.rem(x + o, NX)
        return remote(part(src, xp), win.at[base + x], x_send.at[t, o], x_recv.at[t, NX - o], xdev(o))

    def x_wait(t, o, src, win, base):
        xp = lax.rem(x + o, NX)
        remote(part(src, xp), win.at[base + xp], x_send.at[t, o], x_recv.at[t, o], xdev(o)).wait_recv()

    def y_rows(o, part):
        return pl.ds((o // 2 if part == 0 else 1 - o // 2) * (BLK // 2), BLK // 2)

    def y_copy(o, part):
        block = dyw.at[x, y_rows(NX - o, part)]
        there = (NX - o) // 2 * 2 + part
        return remote(block, block, y_send.at[o // 2 * 2 + part], y_recv.at[there], xdev(o))

    def y_wait(o, part):
        block = dyw.at[lax.rem(x + o, NX), y_rows(o, part)]
        here = o // 2 * 2 + part
        remote(block, block, y_send.at[here], y_recv.at[here], xdev(o)).wait_recv()

    def y_relay(o):
        block = dyw.at[lax.rem(x + o, NX), y_rows(o, 0)]
        return remote(block, block, y_send.at[4 + o // 2], y_recv.at[4 + o // 2], xdev(NX - o))

    def y_relay_wait(o):
        block = dyw.at[lax.rem(x + 2, NX), y_rows(o, 0)]
        remote(block, block, y_send.at[4 + o // 2], y_recv.at[4 + o // 2], xdev(NX - o)).wait_recv()

    mine = pl.ds(pl.multiple_of(FEAT * x, 32), FEAT)
    loads[0].wait()
    turn(kin, ksend)
    pl.semaphore_wait(barrier, 2 * (NX - 1) + 3 + to_reducers + to_owners)
    for o in order:
        x_copy(0, o, ksend, kwin, REACH).start()
    loads[1].wait()
    turn(vin, vsend)
    for o in order:
        x_copy(1, o, vsend, vwin, REACH).start()
    loads[2].wait()
    turn(qin, qsend)
    for o in order:
        x_copy(2, o, qsend, qwin, 0).start()
    loads[3].wait()
    for n in range(2):
        for o in (1, 3):
            y_copy(o, n).start()
    kwin[REACH + x] = ksend[mine, :]
    vwin[REACH + x] = vsend[mine, :]
    qwin[x] = qsend[mine, :]

    def z_up(t, xp, win):
        return remote(
            win.at[REACH + xp], win.at[xp + NX + REACH], f_send.at[t, 0, xp], f_recv.at[t, 0, xp], zdev(down)
        )

    def z_down(t, xp, win):
        return remote(win.at[REACH + xp], win.at[xp - 1], f_send.at[t, 1, xp], f_recv.at[t, 1, xp], zdev(up))

    for t, src, win in ((0, ksend, kwin), (1, vsend, vwin)):
        for o in (0,) + order:
            xp = lax.rem(x + o, NX)
            if o:
                x_wait(t, o, src, win, REACH)

            @pl.when(xp < REACH)
            def _():
                z_up(t, xp, win).start()

            @pl.when(xp >= 1)
            def _():
                z_down(t, xp, win).start()

    def unpack(win, slot, t_out, r_out):
        val = win[slot].astype(F32)
        cols = pl.ds(pl.multiple_of(slot * BLK, BLK), BLK)
        for h in range(HPD):
            piece = val[h * HD : (h + 1) * HD]
            t_out[h, :, cols] = piece.astype(BF16)
            if r_out is not None:
                r_out[h, cols, :] = piece.T.astype(BF16)

    def unpack_k(slot, carry):
        unpack(kwin, slot, kt, kr)
        return carry

    def unpack_v(slot, carry):
        unpack(vwin, slot, vt, vr)
        return carry

    def unpack_q(slot, carry):
        unpack(qwin, slot, qt, None)
        return carry

    def halo_wait(t, win):
        for xp in range(REACH):
            z_up(t, xp, win).wait_recv()
            z_down(t, xp + 1, win).wait_recv()

    lax.fori_loop(REACH, REACH + NX, unpack_k, 0)
    halo_wait(0, kwin)
    lax.fori_loop(0, REACH, unpack_k, 0)
    lax.fori_loop(REACH + NX, SLOTS, unpack_k, 0)
    for o in order:
        x_wait(2, o, qsend, qwin, 0)
    lax.fori_loop(0, NX, unpack_q, 0)

    first = (NX * z - REACH) * BLK
    rows = lax.broadcasted_iota(jnp.int32, (BLK, QG), 0)
    ends = []
    total = jnp.int32(0)
    for i in range(NIMG):
        total = total + len_ref[0, i]
        ends.append(total)

    spans = []
    for g in range(NG):
        pos = NX * z * BLK + g * QG + lax.broadcasted_iota(jnp.int32, (8, QG), 1)
        lo = jnp.zeros_like(pos)
        hi = jnp.full_like(pos, TOKENS)
        for e in ends:
            lo = jnp.where(e <= pos, e, lo)
        for e in ends[::-1]:
            hi = jnp.where(e > pos, e, hi)
        spans.append((lo[0:1] - first - g * QG, hi[0:1] - first - g * QG))

    def forward(h, carry):
        for g in range(NG):
            lo, hi = spans[g]
            q_blk = qt[h, :, g * QG : (g + 1) * QG]
            top = jnp.full((1, QG), NEG, F32)
            for c in range(NCH):
                keys = slice(g * QG + c * BLK, g * QG + (c + 1) * BLK)
                s = dot_nn(kr[h, keys, :], q_blk)
                keep = jnp.logical_and(rows >= lo - c * BLK, rows < hi - c * BLK)
                s = jnp.where(keep, s, NEG)
                s_scr[g, c * BLK : (c + 1) * BLK, :] = s
                top = jnp.maximum(top, jnp.max(s, axis=0, keepdims=True))
            norm = jnp.zeros((1, QG), F32)
            for c in range(NCH):
                e = jnp.exp2((s_scr[g, c * BLK : (c + 1) * BLK, :] - top) * (SCALE * LOG2E))
                s_scr[g, c * BLK : (c + 1) * BLK, :] = e
                norm = norm + jnp.sum(e, axis=0, keepdims=True)
            inv = 1.0 / norm
            for c in range(NCH):
                p_scr[g, h, c * BLK : (c + 1) * BLK, :] = (
                    s_scr[g, c * BLK : (c + 1) * BLK, :] * inv
                ).astype(BF16)
        return carry

    def mix(h, carry):
        for g in range(NG):
            mixed = dot_nn(vt[h, :, g * QG : g * QG + KG], p_scr[g, h])
            att[pl.ds(pl.multiple_of(h * HD, 8), HD), g * QG : (g + 1) * QG] = mixed
        return carry

    far = pl.ds(pl.multiple_of(CSTEP * (1 - core), BLK), CHUNK)
    near = pl.ds(pl.multiple_of(CSTEP * core, BLK), CHUNK)
    s0_copy = remote(wp.at[:, :, far], r0, s0_send, s0_recv, twin)

    def s0_begin():
        attended = att[...].astype(BF16)
        for i in range(D // PART):
            cols = slice(i * PART, (i + 1) * PART)
            share = dot_nn(attended, dyw[:, :, cols].reshape(OWN, PART))
            for h in range(HPD):
                wp[h, 0:HD, cols] = share[h * HD : (h + 1) * HD].astype(BF16)
        s0_copy.start()

    def s1_copy(o):
        return remote(
            w1.at[lax.rem(y + o, NY)], r1.at[NY - o], s1_send.at[o], s1_recv.at[NY - o], ydev(o)
        )

    def s1_begin():
        s0_copy.wait_recv()
        for h in range(HPD):
            w1[h] = (wp[h, :, near].astype(F32) + r0[h].astype(F32)).astype(BF16)
        for o in order:
            s1_copy(o).start()

    def s2_copy(r):
        return remote(s2.at[r], r2.at[z], s2_send.at[r], s2_recv.at[z], (dp, NX * r + x))

    def s2_begin():
        over_dp = w1[y].astype(F32)
        for o in order:
            remote(w1.at[0], r1.at[o], s1_send.at[o], s1_recv.at[o], ydev(o)).wait_recv()
            over_dp = over_dp + r1[o].astype(F32)
        for r in range(NRED):
            s2[r] = over_dp[:, r * BLK : (r + 1) * BLK].astype(BF16)
        for r in range(NRED):

            @pl.when(r != z)
            def _():
                s2_copy(r).start()

            @pl.when(r == z)
            def _():
                r2[r] = s2[r]

    def s3_copy(t):
        return remote(s3.at[t], h5.at[z], s3_send.at[t], s3_recv.at[z], (dp, owner[t]))

    def s3_begin():
        @pl.when(reducer)
        def _():
            for r in range(NZ):

                @pl.when(r != z)
                def _():
                    remote(s2.at[0], r2.at[r], s2_send.at[0], s2_recv.at[r], (dp, NX * r + x)).wait_recv()

            over_z = r2[0].astype(F32)
            for r in range(1, NZ):
                over_z = over_z + r2[r].astype(F32)
            tot[0:PADW, :] = over_z * (ALL_TOK ** -0.5)
            tot[PADW:, :] = jnp.zeros((8, BLK), F32)
            for t in range(2):
                s3[t] = tot[t * ROWS : t * ROWS + PADR, :].astype(BF16)
            for t in range(2):

                @pl.when(owner[t] != seq)
                def _():
                    s3_copy(t).start()

                @pl.when(owner[t] == seq)
                def _():
                    h5[z] = s3[t]

    def s4_copy(o):
        return remote(h5, h5, s4_send.at[o], s4_recv.at[NY - o], ydev(o))

    def s4_begin():
        @pl.when(collector)
        def _():
            for r in range(NRED):

                @pl.when(jnp.logical_not(is_source(r)))
                def _():
                    remote(s3.at[0], h5.at[r], s3_send.at[0], s3_recv.at[r], (dp, NX * r + src_x)).wait_recv()

            for o in order:
                s4_copy(o).start()

    s5_copy = remote(h5, r3.at[core], s5_send, s5_recv, twin)

    def s5_begin():
        for o in order:

            @pl.when(lax.rem(y + o, NY) == src_y)
            def _():
                remote(h5, h5, s4_send.at[o], s4_recv.at[o], ydev(o)).wait_recv()

        s5_copy.start()
        r3[core] = h5[...]

    def backward(h, i, pair):
        feats = slice(i * HD, (i + 1) * HD)
        for g in range(NG):
            cols = slice(g * QG, (g + 1) * QG)
            q_blk, d_blk, p_all = qt[h, :, cols], dt[h, :, cols], p_scr[g, h]
            mixed = att[h * HD : (h + 1) * HD, cols].astype(BF16).astype(F32)
            delta = jnp.sum(d_blk.astype(F32) * mixed, axis=0, keepdims=True)
            for c in range(NCH):
                keys = slice(g * QG + c * BLK, g * QG + (c + 1) * BLK)
                dp_c = dot_nn(vr[h, keys, :], d_blk)
                p = p_scr[g, h, c * BLK : (c + 1) * BLK, :].astype(F32)
                ds_scr[g, c * BLK : (c + 1) * BLK, :] = (SCALE * p * (dp_c - delta)).astype(BF16)
            ds = ds_scr[g]
            dq_acc[pair, feats, cols] = dot_nn(kt[h, :, g * QG : g * QG + KG], ds)
            for acc, left, right in ((dk_acc, q_blk, ds), (dv_acc, d_blk, p_all)):
                add = dot_nt(left, right)
                if g == 0:
                    acc[pair, feats, 0:KG] = add
                else:
                    old = g * QG + KG - QG
                    acc[pair, feats, g * QG : old] += add[:, 0 : KG - QG]
                    acc[pair, feats, old : old + QG] = add[:, KG - QG :]

    def z_copy(t, p, side):
        stage, rz = ((kh_st, rz_k), (vh_st, rz_v))[t]
        zz = down if side == 0 else up
        slots = pl.ds(side * REACH, REACH)
        return remote(
            stage.at[p, slots], rz.at[p, slots], z_send.at[t, p, side], z_recv.at[t, p, side], zdev(zz)
        )

    returns = ((dq_st, rx_q), (t_k, rx_k), (t_v, rx_v))

    def g_copy(t, p, b):
        stage, rx = returns[t]
        return remote(
            stage.at[p, b], rx.at[x, pl.ds(PF * p, PF)], g_send.at[t, p, b], g_recv.at[t, p, x], (dp, NX * z + b)
        )

    def g_start(t, p, b):
        stage, rx = returns[t]

        @pl.when(b != x)
        def _():
            g_copy(t, p, b).start()

        @pl.when(b == x)
        def _():
            rx[b, PF * p : PF * (p + 1), :] = stage[p, b]

    def g_wait(t, p):
        stage, rx = returns[t]
        for b in range(NX):

            @pl.when(b != x)
            def _():
                remote(
                    stage.at[p, b], rx.at[b, pl.ds(PF * p, PF)], g_send.at[t, p, b], g_recv.at[t, p, b],
                    (dp, NX * z + b),
                ).wait_recv()

    def halo_send(p):
        for t, acc, stage in ((0, dk_acc, kh_st), (1, dv_acc, vh_st)):
            for side in range(2):
                for i in range(REACH):
                    slot = i + side * (NX + REACH)
                    stage[p, side * REACH + i] = acc[p, :, slot * BLK : (slot + 1) * BLK].astype(BF16)
                z_copy(t, p, side).start()
        for b in range(NX):
            dq_st[p, b] = dq_acc[p, :, b * BLK : (b + 1) * BLK].astype(BF16)
            g_start(0, p, b)

    def halo_add(p):
        for t, acc, rz in ((0, dk_acc, rz_k), (1, dv_acc, rz_v)):
            for side in range(2):
                z_copy(t, p, side).wait_recv()
            stage = returns[1 + t][0]
            for b in range(NX):
                val = acc[p, :, (REACH + b) * BLK : (REACH + b + 1) * BLK]
                if b >= 1:
                    val = val + rz[p, b - 1].astype(F32)
                if b < REACH:
                    val = val + rz[p, REACH + b].astype(F32)
                stage[p, b] = val.astype(BF16)
                g_start(1 + t, p, b)

    wp[...] = jnp.zeros_like(wp)
    lax.fori_loop(0, PAIRS, forward, 0)
    for o in (1, 3):
        y_wait(o, 0)
        y_relay(o).start()
    lax.fori_loop(PAIRS, HPD, forward, 0)
    lax.fori_loop(REACH, REACH + NX, unpack_v, 0)
    halo_wait(1, vwin)
    lax.fori_loop(0, REACH, unpack_v, 0)
    lax.fori_loop(REACH + NX, SLOTS, unpack_v, 0)
    lax.fori_loop(0, HPD, mix, 0)
    for o in (1, 3):
        y_wait(o, 1)
    for o in (1, 3):
        y_relay_wait(o)
    s0_begin()
    loads[4].wait()
    for g in range(NG):
        d_blk = dot_nt(wbuf[...], dyw[g * 2 : g * 2 + 2].reshape(QG, D))
        for h in range(HPD):
            dt[h, :, g * QG : (g + 1) * QG] = d_blk[h * HD : (h + 1) * HD].astype(BF16)
    s1_begin()
    backward(0, 0, 0)
    backward(1, 1, 0)
    halo_send(0)
    backward(2, 0, 1)
    backward(3, 1, 1)
    s2_begin()
    s3_begin()
    halo_send(1)
    halo_add(0)
    s4_begin()
    halo_add(1)
    s5_begin()

    for t in range(3):
        for p in range(PAIRS):
            g_wait(t, p)
    for o in order:
        x_copy(0, o, ksend, kwin, REACH).wait_send()
        x_copy(1, o, vsend, vwin, REACH).wait_send()
        x_copy(2, o, qsend, qwin, 0).wait_send()
    for o in (1, 3):
        y_copy(o, 0).wait_send()
        y_copy(o, 1).wait_send()
        y_relay(o).wait_send()
    for t, win in ((0, kwin), (1, vwin)):
        for xp in range(REACH):
            z_up(t, xp, win).wait_send()
            z_down(t, xp + 1, win).wait_send()
    for t in range(2):
        for p in range(PAIRS):
            for side in range(2):
                z_copy(t, p, side).wait_send()
    for t in range(3):
        for p in range(PAIRS):
            for b in range(NX):

                @pl.when(b != x)
                def _():
                    g_copy(t, p, b).wait_send()

    s0_copy.wait_send()
    for o in order:
        s1_copy(o).wait_send()
    for r in range(NRED):

        @pl.when(r != z)
        def _():
            s2_copy(r).wait_send()

    @pl.when(reducer)
    def _():
        for t in range(2):

            @pl.when(owner[t] != seq)
            def _():
                s3_copy(t).wait_send()

    @pl.when(collector)
    def _():
        for o in order:
            s4_copy(o).wait_send()

    remote(h5, r3.at[1 - core], s5_send, s5_recv, twin).wait()


def main_call(lengths, queries, keys, values, out_grad, out_weight):
    dma = pltpu.SemaphoreType.DMA
    b16 = lambda *shape: pltpu.VMEM(shape, BF16)
    f32 = lambda *shape: pltpu.VMEM(shape, F32)
    back = jax.ShapeDtypeStruct((NX, FEAT, BLK), BF16)
    return pl.pallas_call(
        main_kernel,
        out_shape=(back, back, back, jax.ShapeDtypeStruct((NCORE, NRED, PADR, BLK), BF16)),
        in_specs=[pl.BlockSpec(memory_space=pltpu.SMEM)] + [HB] * 5,
        out_specs=(VM,) * 4,
        scratch_shapes=[
            b16(BLK, D), b16(BLK, D), b16(BLK, D), b16(FEAT, D), b16(NX, BLK, D),
            b16(D, BLK), b16(D, BLK), b16(D, BLK),
            b16(SLOTS, FEAT, BLK), b16(SLOTS, FEAT, BLK), b16(NX, FEAT, BLK),
            b16(HPD, HD, OWN), b16(HPD, HD, WIDE), b16(HPD, HD, WIDE), b16(HPD, WIDE, HD), b16(HPD, WIDE, HD),
            b16(HPD, HD, OWN),
            f32(NG, KG, QG), b16(NG, HPD, KG, QG), b16(NG, KG, QG), f32(FEAT, OWN),
            f32(PAIRS, PF, OWN), f32(PAIRS, PF, WIDE), f32(PAIRS, PF, WIDE),
            b16(PAIRS, NX, PF, BLK), b16(PAIRS, 2 * REACH, PF, BLK), b16(PAIRS, 2 * REACH, PF, BLK),
            b16(PAIRS, 2 * REACH, PF, BLK), b16(PAIRS, 2 * REACH, PF, BLK),
            b16(PAIRS, NX, PF, BLK), b16(PAIRS, NX, PF, BLK),
            b16(HPD, PADW, D), b16(HPD, PADW, CHUNK), b16(HPD, PADW, CHUNK), b16(NY, PADW, CHUNK),
            b16(NRED, PADW, BLK), b16(NZ, PADW, BLK), f32(PADW + 8, BLK), b16(2, PADR, BLK), b16(NRED, PADR, BLK),
            dma((5,)), dma((3, NX)), dma((3, NX)), dma((6,)), dma((6,)), dma((2, 2, NX)), dma((2, 2, NX)),
            dma((2, PAIRS, 2)), dma((2, PAIRS, 2)), dma((3, PAIRS, NX)), dma((3, PAIRS, NX)),
            dma, dma, dma((NY,)), dma((NY,)), dma((NRED,)), dma((NZ,)), dma((2,)), dma((NRED,)),
            dma((NY,)), dma((NY,)), dma, dma,
        ],
        compiler_params=pltpu.CompilerParams(
            collective_id=0, has_side_effects=True, vmem_limit_bytes=60 * 2**20
        ),
        name="attention_backward",
    )(lengths, queries, keys, values, out_grad, out_weight)


def finish_kernel(rq, rk, rv, rw, gq, gk, gv, gw, inb, outb, wbuf, i_sem, o_sem):
    gets = [pltpu.make_async_copy(r, inb.at[t], i_sem.at[t]) for t, r in enumerate((rq, rk, rv))]
    puts = [pltpu.make_async_copy(outb.at[t], g.at[0], o_sem.at[t]) for t, g in enumerate((gq, gk, gv))]
    for copy in gets:
        copy.start()
    for t in range(3):
        gets[t].wait()
        for i in range(D // BLK):
            outb[t, :, i * BLK : (i + 1) * BLK] = inb[t, i * BLK : (i + 1) * BLK, :].astype(F32).T
        puts[t].start()
    for c in range(NCORE):
        for r in range(NRED):
            col = c * CSTEP + r * BLK
            wbuf[:, col : col + BLK] = rw[c, r, 0:ROWS, :].astype(F32)
    last = pltpu.make_async_copy(wbuf, gw, o_sem.at[3])
    last.start()
    for copy in puts:
        copy.wait()
    last.wait()


def finish(rq, rk, rv, rw):
    grad = jax.ShapeDtypeStruct((1, BLK, D), F32)
    return pl.pallas_call(
        finish_kernel,
        out_shape=(grad, grad, grad, jax.ShapeDtypeStruct((ROWS, D), F32)),
        in_specs=[HB] * 3 + [VM],
        out_specs=(HB,) * 4,
        scratch_shapes=[
            pltpu.VMEM((3, D, BLK), BF16), pltpu.VMEM((3, BLK, D), F32), pltpu.VMEM((ROWS, D), F32),
            pltpu.SemaphoreType.DMA((3,)), pltpu.SemaphoreType.DMA((4,)),
        ],
        name="outputs",
    )(*[r.reshape(D, BLK) for r in (rq, rk, rv)], rw)


def body(queries, keys, values, out_weight, out_grad, lengths):
    return finish(*main_call(lengths, queries, keys, values, out_grad, out_weight))


def solution(mesh):
    rows = P("dp", "seq", None)
    return jax.shard_map(
        body,
        mesh=mesh,
        in_specs=(rows, rows, rows, P(), rows, P("dp", None)),
        out_specs=(rows, rows, rows, P("seq", None)),
        check_vma=False,
    )
```

```python
import math

import jax
import jax.numpy as jnp
from jax import lax
from jax.experimental import pallas as pl
from jax.experimental.pallas import tpu as pltpu
from jax.sharding import PartitionSpec as P

NX, NZ = 4, 8
NY, NCORE = 4, 2
NDP = NY * NCORE
BLK = 128
HEADS, HD = 16, 72
HPD = HEADS // NX
FEAT = HPD * HD
D = HEADS * HD
REACH = 3
SLOTS = NX + 2 * REACH
WIDE = SLOTS * BLK
OWN = NX * BLK
NIMG = 20
TOKENS = 4096
ALL_TOK = 32768
SCALE = HD ** -0.5
LOG2E = math.log2(math.e)
NEG = -1e30
QG = 256
NG = OWN // QG
KG = QG + 2 * REACH * BLK
NCH = KG // BLK
PAIRS = HPD // 2
PART = 3 * BLK
PF = 2 * HD
PADW = 80
CHUNK = 640
CSTEP = 512
NRED = 5
ROWS = D // (NX * NZ)
PADR = 48

F32, BF16 = jnp.float32, jnp.bfloat16
MESH = pl.DeviceIdType.MESH
VM = pl.BlockSpec(memory_space=pltpu.VMEM)
HB = pl.BlockSpec(memory_space=pltpu.HBM)


def remote(src, dst, send, recv, device):
    return pltpu.make_async_remote_copy(
        src_ref=src, dst_ref=dst, send_sem=send, recv_sem=recv, device_id=device, device_id_type=MESH
    )


def hello(barrier, device):
    pl.semaphore_signal(barrier, inc=1, device_id=device, device_id_type=MESH)


def dot_nn(a, b):
    return lax.dot_general(a, b, (((1,), (0,)), ((), ())), preferred_element_type=F32)


def dot_nt(a, b):
    return lax.dot_general(a, b, (((1,), (1,)), ((), ())), preferred_element_type=F32)


def main_kernel(
    len_ref, q_hbm, k_hbm, v_hbm, dy_hbm, w_hbm,
    rx_q, rx_k, rx_v, r3,
    kin, vin, qin, wbuf, dyw, ksend, vsend, qsend, kwin, vwin, qwin,
    qt, kt, vt, kr, vr, dt, s_scr, p_scr, ds_scr, att, dq_acc, dk_acc, dv_acc,
    dq_st, kh_st, vh_st, rz_k, rz_v, t_k, t_v,
    wp, r0, w1, r1, s2, r2, tot, s3, h5,
    l_sem, x_send, x_recv, y_send, y_recv, f_send, f_recv, z_send, z_recv, g_send, g_recv,
    s0_send, s0_recv, s1_send, s1_recv, s2_send, s2_recv, s3_send, s3_recv, s4_send, s4_recv, s5_send, s5_recv,
):
    dp, seq = lax.axis_index("dp"), lax.axis_index("seq")
    z, x = lax.div(seq, NX), lax.rem(seq, NX)
    y, core = lax.div(dp, NCORE), lax.rem(dp, NCORE)
    up, down = lax.rem(z + 1, NZ), lax.rem(z + NZ - 1, NZ)
    barrier = pltpu.get_barrier_semaphore()
    reducer = z < NRED
    order = (1, 3, 2)

    def xdev(o):
        return (dp, NX * z + lax.rem(x + o, NX))

    def zdev(zz):
        return (dp, NX * zz + x)

    def ydev(o):
        return (NCORE * lax.rem(y + o, NY) + core, seq)

    twin = (dp + 1 - 2 * core, seq)

    loads = [
        pltpu.make_async_copy(k_hbm.at[0], kin, l_sem.at[0]),
        pltpu.make_async_copy(v_hbm.at[0], vin, l_sem.at[1]),
        pltpu.make_async_copy(q_hbm.at[0], qin, l_sem.at[2]),
        pltpu.make_async_copy(dy_hbm.at[0], dyw.at[x], l_sem.at[3]),
        pltpu.make_async_copy(w_hbm.at[pl.ds(pl.multiple_of(FEAT * x, 32), FEAT)], wbuf, l_sem.at[4]),
    ]
    for copy in loads:
        copy.start()

    head = HPD * x + y
    owner = [2 * head, 2 * head + 1]
    my_head = lax.div(seq, 2)
    src_x, src_y = lax.div(my_head, HPD), lax.rem(my_head, HPD)
    collector = src_y == y

    def is_source(r):
        return jnp.logical_and(src_x == x, z == r)

    for o in order:
        hello(barrier, xdev(o))
    for zz in (up, down):
        hello(barrier, zdev(zz))
    hello(barrier, twin)
    for o in order:
        hello(barrier, ydev(o))

    @pl.when(reducer)
    def _():
        for o in range(1, NZ):
            hello(barrier, zdev(lax.rem(z + o, NZ)))

    for r in range(NRED):

        @pl.when(jnp.logical_and(collector, jnp.logical_not(is_source(r))))
        def _():
            hello(barrier, (dp, NX * r + src_x))

    to_reducers = jnp.where(reducer, NRED - 1, NRED)
    mine_too = jnp.int32(0)
    for t in range(2):
        mine_too = mine_too + jnp.where(owner[t] == seq, 1, 0)
    to_owners = jnp.where(reducer, 2 - mine_too, 0)

    def turn(src, dst):
        for i in range(D // BLK):
            tile = src[:, i * BLK : (i + 1) * BLK].astype(F32)
            dst[i * BLK : (i + 1) * BLK, :] = tile.T.astype(BF16)

    def part(ref, xp):
        return ref.at[pl.ds(pl.multiple_of(FEAT * xp, 32), FEAT)]

    def x_copy(t, o, src, win, base):
        xp = lax.rem(x + o, NX)
        return remote(part(src, xp), win.at[base + x], x_send.at[t, o], x_recv.at[t, NX - o], xdev(o))

    def x_wait(t, o, src, win, base):
        xp = lax.rem(x + o, NX)
        remote(part(src, xp), win.at[base + xp], x_send.at[t, o], x_recv.at[t, o], xdev(o)).wait_recv()

    def y_rows(o, part):
        return pl.ds((o // 2 if part == 0 else 1 - o // 2) * (BLK // 2), BLK // 2)

    def y_copy(o, part):
        block = dyw.at[x, y_rows(NX - o, part)]
        there = (NX - o) // 2 * 2 + part
        return remote(block, block, y_send.at[o // 2 * 2 + part], y_recv.at[there], xdev(o))

    def y_wait(o, part):
        block = dyw.at[lax.rem(x + o, NX), y_rows(o, part)]
        here = o // 2 * 2 + part
        remote(block, block, y_send.at[here], y_recv.at[here], xdev(o)).wait_recv()

    def y_relay(o):
        block = dyw.at[lax.rem(x + o, NX), y_rows(o, 0)]
        return remote(block, block, y_send.at[4 + o // 2], y_recv.at[4 + o // 2], xdev(NX - o))

    def y_relay_wait(o):
        block = dyw.at[lax.rem(x + 2, NX), y_rows(o, 0)]
        remote(block, block, y_send.at[4 + o // 2], y_recv.at[4 + o // 2], xdev(NX - o)).wait_recv()

    mine = pl.ds(pl.multiple_of(FEAT * x, 32), FEAT)
    loads[0].wait()
    turn(kin, ksend)
    pl.semaphore_wait(barrier, 2 * (NX - 1) + 3 + to_reducers + to_owners)
    for o in order:
        x_copy(0, o, ksend, kwin, REACH).start()
    loads[1].wait()
    turn(vin, vsend)
    for o in order:
        x_copy(1, o, vsend, vwin, REACH).start()
    loads[2].wait()
    turn(qin, qsend)
    for o in order:
        x_copy(2, o, qsend, qwin, 0).start()
    loads[3].wait()
    for n in range(2):
        for o in (1, 3):
            y_copy(o, n).start()
    kwin[REACH + x] = ksend[mine, :]
    vwin[REACH + x] = vsend[mine, :]
    qwin[x] = qsend[mine, :]

    def z_up(t, xp, win):
        return remote(
            win.at[REACH + xp], win.at[xp + NX + REACH], f_send.at[t, 0, xp], f_recv.at[t, 0, xp], zdev(down)
        )

    def z_down(t, xp, win):
        return remote(win.at[REACH + xp], win.at[xp - 1], f_send.at[t, 1, xp], f_recv.at[t, 1, xp], zdev(up))

    for t, src, win in ((0, ksend, kwin), (1, vsend, vwin)):
        for o in (0,) + order:
            xp = lax.rem(x + o, NX)
            if o:
                x_wait(t, o, src, win, REACH)

            @pl.when(xp < REACH)
            def _():
                z_up(t, xp, win).start()

            @pl.when(xp >= 1)
            def _():
                z_down(t, xp, win).start()

    def unpack(win, slot, t_out, r_out):
        val = win[slot].astype(F32)
        cols = pl.ds(pl.multiple_of(slot * BLK, BLK), BLK)
        for h in range(HPD):
            piece = val[h * HD : (h + 1) * HD]
            t_out[h, :, cols] = piece.astype(BF16)
            if r_out is not None:
                r_out[h, cols, :] = piece.T.astype(BF16)

    def unpack_k(slot, carry):
        unpack(kwin, slot, kt, kr)
        return carry

    def unpack_v(slot, carry):
        unpack(vwin, slot, vt, vr)
        return carry

    def unpack_q(slot, carry):
        unpack(qwin, slot, qt, None)
        return carry

    def halo_wait(t, win):
        for xp in range(REACH):
            z_up(t, xp, win).wait_recv()
            z_down(t, xp + 1, win).wait_recv()

    lax.fori_loop(REACH, REACH + NX, unpack_k, 0)
    halo_wait(0, kwin)
    lax.fori_loop(0, REACH, unpack_k, 0)
    lax.fori_loop(REACH + NX, SLOTS, unpack_k, 0)
    for o in order:
        x_wait(2, o, qsend, qwin, 0)
    lax.fori_loop(0, NX, unpack_q, 0)

    first = (NX * z - REACH) * BLK
    rows = lax.broadcasted_iota(jnp.int32, (BLK, QG), 0)
    ends = []
    total = jnp.int32(0)
    for i in range(NIMG):
        total = total + len_ref[0, i]
        ends.append(total)

    spans = []
    for g in range(NG):
        pos = NX * z * BLK + g * QG + lax.broadcasted_iota(jnp.int32, (8, QG), 1)
        lo = jnp.zeros_like(pos)
        hi = jnp.full_like(pos, TOKENS)
        for e in ends:
            lo = jnp.where(e <= pos, e, lo)
        for e in ends[::-1]:
            hi = jnp.where(e > pos, e, hi)
        spans.append((lo[0:1] - first - g * QG, hi[0:1] - first - g * QG))

    def forward(h, carry):
        for g in range(NG):
            lo, hi = spans[g]
            q_blk = qt[h, :, g * QG : (g + 1) * QG]
            top = jnp.full((1, QG), NEG, F32)
            for c in range(NCH):
                keys = slice(g * QG + c * BLK, g * QG + (c + 1) * BLK)
                s = dot_nn(kr[h, keys, :], q_blk)
                keep = jnp.logical_and(rows >= lo - c * BLK, rows < hi - c * BLK)
                s = jnp.where(keep, s, NEG)
                s_scr[g, c * BLK : (c + 1) * BLK, :] = s
                top = jnp.maximum(top, jnp.max(s, axis=0, keepdims=True))
            norm = jnp.zeros((1, QG), F32)
            for c in range(NCH):
                e = jnp.exp2((s_scr[g, c * BLK : (c + 1) * BLK, :] - top) * (SCALE * LOG2E))
                s_scr[g, c * BLK : (c + 1) * BLK, :] = e
                norm = norm + jnp.sum(e, axis=0, keepdims=True)
            inv = 1.0 / norm
            for c in range(NCH):
                p_scr[g, h, c * BLK : (c + 1) * BLK, :] = (
                    s_scr[g, c * BLK : (c + 1) * BLK, :] * inv
                ).astype(BF16)
        return carry

    def mix(h, carry):
        for g in range(NG):
            mixed = dot_nn(vt[h, :, g * QG : g * QG + KG], p_scr[g, h])
            att[pl.ds(pl.multiple_of(h * HD, 8), HD), g * QG : (g + 1) * QG] = mixed
        return carry

    far = pl.ds(pl.multiple_of(CSTEP * (1 - core), BLK), CHUNK)
    near = pl.ds(pl.multiple_of(CSTEP * core, BLK), CHUNK)
    s0_copy = remote(wp.at[:, :, far], r0, s0_send, s0_recv, twin)

    def s0_begin():
        attended = att[...].astype(BF16)
        for i in range(D // PART):
            cols = slice(i * PART, (i + 1) * PART)
            share = dot_nn(attended, dyw[:, :, cols].reshape(OWN, PART))
            for h in range(HPD):
                wp[h, 0:HD, cols] = share[h * HD : (h + 1) * HD].astype(BF16)
        s0_copy.start()

    def s1_copy(o):
        return remote(
            w1.at[lax.rem(y + o, NY)], r1.at[NY - o], s1_send.at[o], s1_recv.at[NY - o], ydev(o)
        )

    def s1_begin():
        s0_copy.wait_recv()
        for h in range(HPD):
            w1[h] = (wp[h, :, near].astype(F32) + r0[h].astype(F32)).astype(BF16)
        for o in order:
            s1_copy(o).start()

    def s2_copy(r):
        return remote(s2.at[r], r2.at[z], s2_send.at[r], s2_recv.at[z], (dp, NX * r + x))

    def s2_begin():
        over_dp = w1[y].astype(F32)
        for o in order:
            remote(w1.at[0], r1.at[o], s1_send.at[o], s1_recv.at[o], ydev(o)).wait_recv()
            over_dp = over_dp + r1[o].astype(F32)
        for r in range(NRED):
            s2[r] = over_dp[:, r * BLK : (r + 1) * BLK].astype(BF16)
        for r in range(NRED):

            @pl.when(r != z)
            def _():
                s2_copy(r).start()

            @pl.when(r == z)
            def _():
                r2[r] = s2[r]

    def s3_copy(t):
        return remote(s3.at[t], h5.at[z], s3_send.at[t], s3_recv.at[z], (dp, owner[t]))

    def s3_begin():
        @pl.when(reducer)
        def _():
            for r in range(NZ):

                @pl.when(r != z)
                def _():
                    remote(s2.at[0], r2.at[r], s2_send.at[0], s2_recv.at[r], (dp, NX * r + x)).wait_recv()

            over_z = r2[0].astype(F32)
            for r in range(1, NZ):
                over_z = over_z + r2[r].astype(F32)
            tot[0:PADW, :] = over_z * (ALL_TOK ** -0.5)
            tot[PADW:, :] = jnp.zeros((8, BLK), F32)
            for t in range(2):
                s3[t] = tot[t * ROWS : t * ROWS + PADR, :].astype(BF16)
            for t in range(2):

                @pl.when(owner[t] != seq)
                def _():
                    s3_copy(t).start()

                @pl.when(owner[t] == seq)
                def _():
                    h5[z] = s3[t]

    def s4_copy(o):
        return remote(h5, h5, s4_send.at[o], s4_recv.at[NY - o], ydev(o))

    def s4_begin():
        @pl.when(collector)
        def _():
            for r in range(NRED):

                @pl.when(jnp.logical_not(is_source(r)))
                def _():
                    remote(s3.at[0], h5.at[r], s3_send.at[0], s3_recv.at[r], (dp, NX * r + src_x)).wait_recv()

            for o in order:
                s4_copy(o).start()

    s5_copy = remote(h5, r3.at[core], s5_send, s5_recv, twin)

    def s5_begin():
        for o in order:

            @pl.when(lax.rem(y + o, NY) == src_y)
            def _():
                remote(h5, h5, s4_send.at[o], s4_recv.at[o], ydev(o)).wait_recv()

        s5_copy.start()
        r3[core] = h5[...]

    def backward(h, i, pair):
        feats = slice(i * HD, (i + 1) * HD)
        for g in range(NG):
            cols = slice(g * QG, (g + 1) * QG)
            q_blk, d_blk, p_all = qt[h, :, cols], dt[h, :, cols], p_scr[g, h]
            mixed = att[h * HD : (h + 1) * HD, cols].astype(BF16).astype(F32)
            delta = jnp.sum(d_blk.astype(F32) * mixed, axis=0, keepdims=True)
            for c in range(NCH):
                keys = slice(g * QG + c * BLK, g * QG + (c + 1) * BLK)
                dp_c = dot_nn(vr[h, keys, :], d_blk)
                p = p_scr[g, h, c * BLK : (c + 1) * BLK, :].astype(F32)
                ds_scr[g, c * BLK : (c + 1) * BLK, :] = (SCALE * p * (dp_c - delta)).astype(BF16)
            ds = ds_scr[g]
            dq_acc[pair, feats, cols] = dot_nn(kt[h, :, g * QG : g * QG + KG], ds)
            for acc, left, right in ((dk_acc, q_blk, ds), (dv_acc, d_blk, p_all)):
                add = dot_nt(left, right)
                if g == 0:
                    acc[pair, feats, 0:KG] = add
                else:
                    old = g * QG + KG - QG
                    acc[pair, feats, g * QG : old] += add[:, 0 : KG - QG]
                    acc[pair, feats, old : old + QG] = add[:, KG - QG :]

    def z_copy(t, p, side):
        stage, rz = ((kh_st, rz_k), (vh_st, rz_v))[t]
        zz = down if side == 0 else up
        slots = pl.ds(side * REACH, REACH)
        return remote(
            stage.at[p, slots], rz.at[p, slots], z_send.at[t, p, side], z_recv.at[t, p, side], zdev(zz)
        )

    returns = ((dq_st, rx_q), (t_k, rx_k), (t_v, rx_v))

    def g_copy(t, p, b):
        stage, rx = returns[t]
        return remote(
            stage.at[p, b], rx.at[x, pl.ds(PF * p, PF)], g_send.at[t, p, b], g_recv.at[t, p, x], (dp, NX * z + b)
        )

    def g_start(t, p, b):
        stage, rx = returns[t]

        @pl.when(b != x)
        def _():
            g_copy(t, p, b).start()

        @pl.when(b == x)
        def _():
            rx[b, PF * p : PF * (p + 1), :] = stage[p, b]

    def g_wait(t, p):
        stage, rx = returns[t]
        for b in range(NX):

            @pl.when(b != x)
            def _():
                remote(
                    stage.at[p, b], rx.at[b, pl.ds(PF * p, PF)], g_send.at[t, p, b], g_recv.at[t, p, b],
                    (dp, NX * z + b),
                ).wait_recv()

    def halo_send(p):
        for t, acc, stage in ((0, dk_acc, kh_st), (1, dv_acc, vh_st)):
            for side in range(2):
                for i in range(REACH):
                    slot = i + side * (NX + REACH)
                    stage[p, side * REACH + i] = acc[p, :, slot * BLK : (slot + 1) * BLK].astype(BF16)
                z_copy(t, p, side).start()
        for b in range(NX):
            dq_st[p, b] = dq_acc[p, :, b * BLK : (b + 1) * BLK].astype(BF16)
            g_start(0, p, b)

    def halo_add(p):
        for t, acc, rz in ((0, dk_acc, rz_k), (1, dv_acc, rz_v)):
            for side in range(2):
                z_copy(t, p, side).wait_recv()
            stage = returns[1 + t][0]
            for b in range(NX):
                val = acc[p, :, (REACH + b) * BLK : (REACH + b + 1) * BLK]
                if b >= 1:
                    val = val + rz[p, b - 1].astype(F32)
                if b < REACH:
                    val = val + rz[p, REACH + b].astype(F32)
                stage[p, b] = val.astype(BF16)
                g_start(1 + t, p, b)

    wp[...] = jnp.zeros_like(wp)
    lax.fori_loop(0, PAIRS, forward, 0)
    for o in (1, 3):
        y_wait(o, 0)
        y_relay(o).start()
    lax.fori_loop(PAIRS, HPD, forward, 0)
    lax.fori_loop(REACH, REACH + NX, unpack_v, 0)
    halo_wait(1, vwin)
    lax.fori_loop(0, REACH, unpack_v, 0)
    lax.fori_loop(REACH + NX, SLOTS, unpack_v, 0)
    lax.fori_loop(0, HPD, mix, 0)
    for o in (1, 3):
        y_wait(o, 1)
    for o in (1, 3):
        y_relay_wait(o)
    s0_begin()
    loads[4].wait()
    for g in range(NG):
        d_blk = dot_nt(wbuf[...], dyw[g * 2 : g * 2 + 2].reshape(QG, D))
        for h in range(HPD):
            dt[h, :, g * QG : (g + 1) * QG] = d_blk[h * HD : (h + 1) * HD].astype(BF16)
    s1_begin()
    backward(0, 0, 0)
    backward(1, 1, 0)
    halo_send(0)
    backward(2, 0, 1)
    backward(3, 1, 1)
    s2_begin()
    s3_begin()
    halo_send(1)
    s4_begin()
    halo_add(0)
    halo_add(1)
    s5_begin()

    for t in range(3):
        for p in range(PAIRS):
            g_wait(t, p)
    for o in order:
        x_copy(0, o, ksend, kwin, REACH).wait_send()
        x_copy(1, o, vsend, vwin, REACH).wait_send()
        x_copy(2, o, qsend, qwin, 0).wait_send()
    for o in (1, 3):
        y_copy(o, 0).wait_send()
        y_copy(o, 1).wait_send()
        y_relay(o).wait_send()
    for t, win in ((0, kwin), (1, vwin)):
        for xp in range(REACH):
            z_up(t, xp, win).wait_send()
            z_down(t, xp + 1, win).wait_send()
    for t in range(2):
        for p in range(PAIRS):
            for side in range(2):
                z_copy(t, p, side).wait_send()
    for t in range(3):
        for p in range(PAIRS):
            for b in range(NX):

                @pl.when(b != x)
                def _():
                    g_copy(t, p, b).wait_send()

    s0_copy.wait_send()
    for o in order:
        s1_copy(o).wait_send()
    for r in range(NRED):

        @pl.when(r != z)
        def _():
            s2_copy(r).wait_send()

    @pl.when(reducer)
    def _():
        for t in range(2):

            @pl.when(owner[t] != seq)
            def _():
                s3_copy(t).wait_send()

    @pl.when(collector)
    def _():
        for o in order:
            s4_copy(o).wait_send()

    remote(h5, r3.at[1 - core], s5_send, s5_recv, twin).wait()


def main_call(lengths, queries, keys, values, out_grad, out_weight):
    dma = pltpu.SemaphoreType.DMA
    b16 = lambda *shape: pltpu.VMEM(shape, BF16)
    f32 = lambda *shape: pltpu.VMEM(shape, F32)
    back = jax.ShapeDtypeStruct((NX, FEAT, BLK), BF16)
    return pl.pallas_call(
        main_kernel,
        out_shape=(back, back, back, jax.ShapeDtypeStruct((NCORE, NRED, PADR, BLK), BF16)),
        in_specs=[pl.BlockSpec(memory_space=pltpu.SMEM)] + [HB] * 5,
        out_specs=(VM,) * 4,
        scratch_shapes=[
            b16(BLK, D), b16(BLK, D), b16(BLK, D), b16(FEAT, D), b16(NX, BLK, D),
            b16(D, BLK), b16(D, BLK), b16(D, BLK),
            b16(SLOTS, FEAT, BLK), b16(SLOTS, FEAT, BLK), b16(NX, FEAT, BLK),
            b16(HPD, HD, OWN), b16(HPD, HD, WIDE), b16(HPD, HD, WIDE), b16(HPD, WIDE, HD), b16(HPD, WIDE, HD),
            b16(HPD, HD, OWN),
            f32(NG, KG, QG), b16(NG, HPD, KG, QG), b16(NG, KG, QG), f32(FEAT, OWN),
            f32(PAIRS, PF, OWN), f32(PAIRS, PF, WIDE), f32(PAIRS, PF, WIDE),
            b16(PAIRS, NX, PF, BLK), b16(PAIRS, 2 * REACH, PF, BLK), b16(PAIRS, 2 * REACH, PF, BLK),
            b16(PAIRS, 2 * REACH, PF, BLK), b16(PAIRS, 2 * REACH, PF, BLK),
            b16(PAIRS, NX, PF, BLK), b16(PAIRS, NX, PF, BLK),
            b16(HPD, PADW, D), b16(HPD, PADW, CHUNK), b16(HPD, PADW, CHUNK), b16(NY, PADW, CHUNK),
            b16(NRED, PADW, BLK), b16(NZ, PADW, BLK), f32(PADW + 8, BLK), b16(2, PADR, BLK), b16(NRED, PADR, BLK),
            dma((5,)), dma((3, NX)), dma((3, NX)), dma((6,)), dma((6,)), dma((2, 2, NX)), dma((2, 2, NX)),
            dma((2, PAIRS, 2)), dma((2, PAIRS, 2)), dma((3, PAIRS, NX)), dma((3, PAIRS, NX)),
            dma, dma, dma((NY,)), dma((NY,)), dma((NRED,)), dma((NZ,)), dma((2,)), dma((NRED,)),
            dma((NY,)), dma((NY,)), dma, dma,
        ],
        compiler_params=pltpu.CompilerParams(
            collective_id=0, has_side_effects=True, vmem_limit_bytes=60 * 2**20
        ),
        name="attention_backward",
    )(lengths, queries, keys, values, out_grad, out_weight)


def finish_kernel(rq, rk, rv, rw, gq, gk, gv, gw, inb, outb, wbuf, i_sem, o_sem):
    gets = [pltpu.make_async_copy(r, inb.at[t], i_sem.at[t]) for t, r in enumerate((rq, rk, rv))]
    puts = [pltpu.make_async_copy(outb.at[t], g.at[0], o_sem.at[t]) for t, g in enumerate((gq, gk, gv))]
    for copy in gets:
        copy.start()
    for t in range(3):
        gets[t].wait()
        for i in range(D // BLK):
            outb[t, :, i * BLK : (i + 1) * BLK] = inb[t, i * BLK : (i + 1) * BLK, :].astype(F32).T
        puts[t].start()
    for c in range(NCORE):
        for r in range(NRED):
            col = c * CSTEP + r * BLK
            wbuf[:, col : col + BLK] = rw[c, r, 0:ROWS, :].astype(F32)
    last = pltpu.make_async_copy(wbuf, gw, o_sem.at[3])
    last.start()
    for copy in puts:
        copy.wait()
    last.wait()


def finish(rq, rk, rv, rw):
    grad = jax.ShapeDtypeStruct((1, BLK, D), F32)
    return pl.pallas_call(
        finish_kernel,
        out_shape=(grad, grad, grad, jax.ShapeDtypeStruct((ROWS, D), F32)),
        in_specs=[HB] * 3 + [VM],
        out_specs=(HB,) * 4,
        scratch_shapes=[
            pltpu.VMEM((3, D, BLK), BF16), pltpu.VMEM((3, BLK, D), F32), pltpu.VMEM((ROWS, D), F32),
            pltpu.SemaphoreType.DMA((3,)), pltpu.SemaphoreType.DMA((4,)),
        ],
        name="outputs",
    )(*[r.reshape(D, BLK) for r in (rq, rk, rv)], rw)


def body(queries, keys, values, out_weight, out_grad, lengths):
    return finish(*main_call(lengths, queries, keys, values, out_grad, out_weight))


def solution(mesh):
    rows = P("dp", "seq", None)
    return jax.shard_map(
        body,
        mesh=mesh,
        in_specs=(rows, rows, rows, P(), rows, P("dp", None)),
        out_specs=(rows, rows, rows, P("seq", None)),
        check_vma=False,
    )
```
